256 devices in a mesh: fsdp: 16 (over y_lo, z), ctx: 16 (over x, y_hi, core).
Axes of the slice: x: 4, y: 4 (y_hi: 2, y_lo: 2; y = y_hi * 2 + y_lo), z: 8, core: 2. Of those that a mesh axis runs over, the one named last changes fastest.
Arguments:
- tokens: bfloat16 [32768, 8192], P('ctx', 'fsdp'), may hold values from -6 to 6
- in_proj: bfloat16 [3, 8192, 1024], P(None, 'fsdp', 'ctx'), may hold values from -0.09375 to 0.09375
- filter_taps: float32 [1024, 32768], P('fsdp', 'ctx'), may hold values from -0.7 to 0.7
- skip_gain: float32 [1024], P('fsdp'), may hold values from -4 to 4
- out_proj: bfloat16 [1024, 8192], P('ctx', 'fsdp'), may hold values from -0.1875 to 0.1875
Outputs:
- projected: bfloat16 [32768, 8192], P('ctx', 'fsdp')
The draws below stay inside these ranges and needn't reach their ends.
All inputs are finite; a program needn't handle non-finite values.
Results may differ from the reference program's by a relative error of at most 0.038.
Values may be sent and summed in bfloat16 or wider, within the bound.
No kernel may reach another device: no remote copies, remote signals or barrier semaphores. Data moves between devices by JAX's collectives and lax.ppermute only.
A program may use at most 128 MiB of HBM per device.

```python
import math
import jax
import jax.numpy as jnp
from jax import lax

D = 8192
SLAB = 1024
FEAT_DEV = 512
SEQ = 32768


def draw_filter_taps(key, part):
    key = jax.random.fold_in(key, 11)
    rate_key, tap_key = jax.random.split(key)
    lowest = 0.5 / SEQ
    highest = 1.0 / 40.0
    values = jax.random.truncated_normal(tap_key, -3.0, 3.0, (SLAB, SEQ), jnp.float32)
    rates = jnp.exp(jax.random.uniform(rate_key, (SLAB, 1), jnp.float32, math.log(lowest), math.log(highest)))
    places = jnp.arange(SEQ, dtype=jnp.float32)[None, :]
    scaling = jnp.sqrt(1.0 - jnp.exp(-2.0 * rates))
    return values * jnp.exp(-rates * places) * scaling


def strengthened(result, own_key, source, target, blocks, factor):
    def block_of(position):
        return (jnp.arange(result.shape[position]) // (result.shape[position] // blocks)).reshape((-1,) + (1,) * (result.ndim - 1 - position))

    one_side = jax.random.permutation(own_key, blocks)[block_of(target)]
    other_side = (block_of(target) + blocks // 2) % blocks
    return jnp.where((block_of(source) == one_side) | (block_of(source) == other_side), factor * result, result)


def shard_levels(stream_key, dims, cuts, smallest, largest):
    loudness = 1.0
    for axis_at, shards_of in cuts:
        heights = jax.random.uniform(jax.random.fold_in(jax.random.fold_in(stream_key, 6), axis_at), (shards_of,), jnp.float32, smallest / len(cuts), largest / len(cuts))
        loudness = loudness * jnp.repeat(jnp.exp(heights), dims[axis_at] // shards_of).reshape((-1,) + (1,) * (len(dims) - 1 - axis_at))
    return loudness


def centred(stream_key, dims, deviation, reach, pieces=(), kind=jnp.bfloat16):
    array = deviation * jax.random.normal(stream_key, dims, jnp.float32)
    if pieces:
        array = array * shard_levels(stream_key, dims, pieces, -0.22, 0.18)
    return jnp.clip(array, -reach, reach).astype(kind)


def bell_draw_with(stream_key, extent, scale, bound, pieces, heavy, held_as=jnp.bfloat16):
    result = scale * jax.random.normal(stream_key, extent, jnp.float32)
    if pieces:
        result = result * shard_levels(stream_key, extent, pieces, -0.22, 0.18)
    return jnp.clip(strengthened(result, jax.random.fold_in(stream_key, 3), *heavy), -bound, bound).astype(held_as)


def setup_inputs(seed: int = 0) -> dict:
    streams_of = jax.random.split(jax.random.key(seed), 6)
    tokens = centred(streams_of[0], (SEQ, D), 1.0, 6.0, ((0, 16), (1, 16)))
    in_proj = bell_draw_with(streams_of[1], (3, D, SLAB), D ** -0.5, 0.09375, ((1, 16), (2, 16)), (1, 2, 16, 2.0))
    filter_taps = draw_filter_taps(jax.random.fold_in(streams_of[5], 71), 0)
    skip_gain = centred(streams_of[3], (SLAB,), 1.0, 4.0, ((0, 16),), jnp.float32)
    out_proj = centred(streams_of[4], (SLAB, D), SLAB ** -0.5, 0.1875, ((0, 16), (1, 16)))
    return dict(tokens=tokens, in_proj=in_proj, filter_taps=filter_taps, skip_gain=skip_gain, out_proj=out_proj)


def reference(tokens, in_proj, filter_taps, skip_gain, out_proj):
    blocks = D // FEAT_DEV
    token_blocks = tokens.reshape(SEQ, blocks, FEAT_DEV).transpose(1, 0, 2)
    weight_blocks = in_proj.reshape(3, blocks, FEAT_DEV, SLAB).transpose(1, 0, 2, 3)

    def add_block(running, paired):
        token_part = paired[0]
        weight_part = paired[1]
        terms = []
        for stream in range(3):
            rounded = jnp.dot(token_part, weight_part[stream], preferred_element_type=jnp.float32).astype(jnp.bfloat16)
            rounded = lax.optimization_barrier(rounded)
            terms.append(rounded.astype(jnp.float32))
        return running + jnp.stack(terms), jnp.zeros((), jnp.float32)

    running = lax.scan(add_block, jnp.zeros((3, SEQ, SLAB), jnp.float32), (token_blocks, weight_blocks))[0]
    streams = running.astype(jnp.bfloat16)
    query_part = streams[0].astype(jnp.float32)
    key_part = streams[1].astype(jnp.float32)
    value_part = streams[2].astype(jnp.float32)
    mixed_in = key_part * value_part
    signal_spectrum = jnp.fft.rfft(mixed_in, n=2 * SEQ, axis=0)
    filter_spectrum = jnp.fft.rfft(filter_taps.T, n=2 * SEQ, axis=0)
    convolved = jnp.fft.irfft(signal_spectrum * filter_spectrum, n=2 * SEQ, axis=0)[:SEQ].astype(jnp.float32)
    gated_values = (query_part * (convolved + skip_gain[None, :] * mixed_in)).astype(jnp.bfloat16)
    return jnp.dot(gated_values, out_proj, preferred_element_type=jnp.float32).astype(jnp.bfloat16)
```

```python
import math

import jax
import jax.numpy as jnp
import numpy as np
from jax import lax
from jax.experimental import pallas as pl
from jax.experimental.pallas import tpu as pltpu
from jax.sharding import PartitionSpec as P

AXES = ("fsdp", "ctx")
RINGS = 8
SEQ = 32768
ROWS = 128
COLS = 256
F32 = jnp.float32
BF16 = jnp.bfloat16


def flip(array, mask):
    return lax.ppermute(array, AXES, [(i, i ^ mask) for i in range(256)])


FLIP_CORE = 1
FLIP_Y_HI = 2
FLIP_X = 4
FLIP_Y_LO = 128


def along_z(array, step):
    pairs = []
    for i in range(256):
        z = (i // 16) % RINGS
        pairs.append((i, i + 16 * ((z + step) % RINGS - z)))
    return lax.ppermute(array, AXES, pairs)


def plane_groups():
    return [
        [(y_lo * RINGS + z) * 16 + ctx for ctx in range(16) for y_lo in range(2)]
        for z in range(RINGS)
    ]


def transform_tables():
    freq = np.arange(ROWS)[:, None] + 0.25
    row_angle = 2.0 * np.pi * freq * np.arange(ROWS)[None, :] / ROWS
    twiddle_angle = 2.0 * np.pi * freq * np.arange(COLS)[None, :] / SEQ
    col_angle = 2.0 * np.pi * (np.arange(COLS)[:, None] * np.arange(COLS)[None, :] % COLS) / COLS
    cos_col, sin_col = np.cos(col_angle), np.sin(col_angle)
    row_forward = np.concatenate([np.cos(row_angle), -np.sin(row_angle)], axis=0)
    row_inverse = np.concatenate([np.cos(row_angle), -np.sin(row_angle)], axis=0).T / SEQ
    col_forward = np.block([[cos_col, -sin_col], [sin_col, cos_col]])
    col_inverse = np.block([[cos_col, sin_col], [-sin_col, cos_col]])
    twiddle = np.stack([np.cos(twiddle_angle), -np.sin(twiddle_angle)])
    return row_forward, row_inverse, col_forward, col_inverse, twiddle


def row_order(sources):
    per_source = ROWS // sources
    return (np.arange(sources)[None, :] * per_source + np.arange(per_source)[:, None]).reshape(-1)


def dot32(left, right):
    return jnp.dot(left, right, preferred_element_type=F32)


def forward(signal_ref, row_table, col_table, twiddle_ref):
    channels, sources, _ = signal_ref.shape
    per_source = ROWS // sources
    cos_part, sin_part = twiddle_ref[0], twiddle_ref[1]
    turned = []
    for channel in range(channels):
        signal = jnp.concatenate(
            [signal_ref[channel, :, pl.ds(j * COLS, COLS)] for j in range(per_source)], axis=0
        )
        both = dot32(row_table[...], signal)
        real, imag = both[:ROWS], both[ROWS:]
        turned.append(
            jnp.concatenate(
                [
                    (real * cos_part - imag * sin_part).astype(BF16),
                    (real * sin_part + imag * cos_part).astype(BF16),
                ],
                axis=1,
            )
        )
    return dot32(jnp.concatenate(turned, axis=0), col_table[...])


def filter_kernel(taps_ref, row_table, col_table, twiddle_ref, out_ref):
    out_ref[...] = forward(taps_ref, row_table, col_table, twiddle_ref)


def conv_kernel(
    signal_ref, spectrum_ref, row_table, col_table, col_back, row_back, twiddle_ref, out_ref
):
    channels, sources, _ = signal_ref.shape
    per_source = ROWS // sources
    spectrum = forward(signal_ref, row_table, col_table, twiddle_ref)
    real, imag = spectrum[:, :COLS], spectrum[:, COLS:]
    filter_real, filter_imag = spectrum_ref[:, :COLS], spectrum_ref[:, COLS:]
    product = jnp.concatenate(
        [
            (real * filter_real - imag * filter_imag).astype(BF16),
            (real * filter_imag + imag * filter_real).astype(BF16),
        ],
        axis=1,
    )
    back = dot32(product, col_back[...])
    cos_part, sin_part = twiddle_ref[0], twiddle_ref[1]
    for channel in range(channels):
        part = back[channel * ROWS : (channel + 1) * ROWS]
        real, imag = part[:, :COLS], part[:, COLS:]
        turned = jnp.concatenate(
            [
                (real * cos_part + imag * sin_part).astype(BF16),
                (imag * cos_part - real * sin_part).astype(BF16),
            ],
            axis=0,
        )
        result = dot32(row_back[...], turned).astype(BF16)
        for j in range(per_source):
            out_ref[channel, :, pl.ds(j * COLS, COLS)] = result[j * sources : (j + 1) * sources]


def call_local(kernel, out_shape, *operands):
    vmem = pl.BlockSpec(memory_space=pltpu.VMEM)
    return pl.pallas_call(
        kernel,
        out_shape=out_shape,
        in_specs=[vmem] * len(operands),
        out_specs=vmem,
        compiler_params=pltpu.CompilerParams(vmem_limit_bytes=24 * 1024 * 1024),
    )(*operands)


def gather_weights(shard):
    wide = jnp.concatenate([shard, flip(shard, FLIP_Y_LO)], axis=-1)
    wide = jnp.stack(
        [
            wide,
            jnp.concatenate(
                [flip(shard, FLIP_Y_HI), flip(shard, FLIP_Y_HI | FLIP_Y_LO)], axis=-1
            ),
        ]
    )
    wide = jnp.stack([wide] + [flip(wide, FLIP_X * step) for step in (1, 2, 3)])
    other = flip(wide, FLIP_CORE)
    return jnp.stack([wide, other], axis=2).reshape((16,) + shard.shape[:-1] + (1024,))


def local(tokens, in_proj, filter_taps, skip_gain, out_proj):
    fsdp = lax.axis_index("fsdp")
    ctx = lax.axis_index("ctx")
    y_lo, z = fsdp // RINGS, fsdp % RINGS
    groups = plane_groups()
    row_forward, row_inverse, col_forward, col_inverse, twiddle = transform_tables()
    as_bf16 = lambda table: jnp.asarray(table.astype(np.float32)).astype(BF16)
    twiddle = jnp.asarray(twiddle.astype(np.float32))

    half = tokens.shape[0] // 2
    kept = lax.dynamic_slice_in_dim(tokens, y_lo * half, half, 0)
    given = lax.dynamic_slice_in_dim(tokens, (1 - y_lo) * half, half, 0)
    wide_tokens = jnp.concatenate([kept, flip(given, FLIP_Y_LO)], axis=1)

    shards = in_proj.transpose(0, 2, 1)

    def stream_sums(stream):
        weights = gather_weights(shards[stream])
        parts = lax.dot_general(
            weights.reshape(1024, 1024),
            wide_tokens,
            (((1,), (1,)), ((), ())),
            preferred_element_type=F32,
        ).astype(BF16)
        parts = parts.reshape(16, 64, half)

        def piece(offset, which):
            place = (z + offset) % RINGS + RINGS * which
            return lax.dynamic_index_in_dim(parts, ctx ^ place, 0, keepdims=False).astype(F32)

        up = along_z(piece(4, 0).astype(BF16), 1)
        down = along_z(piece(-4, 1).astype(BF16), -1)
        up = jnp.stack([piece(3, 0) + up.astype(F32), piece(3, 1)]).astype(BF16)
        down = jnp.stack([piece(-3, 0), piece(-3, 1) + down.astype(F32)]).astype(BF16)
        for distance in (2, 1):
            up, down = along_z(up, 1), along_z(down, -1)
            up = jnp.stack(
                [piece(distance, which) + up[which].astype(F32) for which in range(2)]
            ).astype(BF16)
            down = jnp.stack(
                [piece(-distance, which) + down[which].astype(F32) for which in range(2)]
            ).astype(BF16)
        up, down = along_z(up, 1), along_z(down, -1)
        return jnp.stack(
            [piece(0, which) + up[which].astype(F32) + down[which].astype(F32) for which in range(2)]
        )

    value = stream_sums(2)
    key = stream_sums(1)
    query = stream_sums(0)
    mixed = key * value

    taps = lax.all_to_all(
        filter_taps.astype(BF16).reshape(16, 4, 2048), "ctx", split_axis=0, concat_axis=0, tiled=True
    ).transpose(1, 0, 2)
    spectrum = call_local(
        filter_kernel,
        jax.ShapeDtypeStruct((4 * ROWS, 2 * COLS), F32),
        taps,
        as_bf16(row_forward[:, row_order(16)]),
        as_bf16(col_forward),
        twiddle,
    )

    def to_plane(array):
        return lax.all_to_all(
            array, AXES, split_axis=0, concat_axis=0, tiled=True, axis_index_groups=groups
        )

    spread = mixed.astype(BF16).reshape(2, 16, 4, half).transpose(1, 0, 2, 3).reshape(32, 4, half)
    spread = to_plane(spread).transpose(1, 0, 2)
    convolved = call_local(
        conv_kernel,
        jax.ShapeDtypeStruct(spread.shape, BF16),
        spread,
        spectrum,
        as_bf16(row_forward[:, row_order(32)]),
        as_bf16(col_forward),
        as_bf16(col_inverse),
        as_bf16(row_inverse[row_order(32)]),
        twiddle,
    )
    convolved = to_plane(convolved.transpose(1, 0, 2))
    convolved = convolved.reshape(16, 2, 4, half).transpose(1, 0, 2, 3).reshape(2, 64, half)

    other_gain = flip(skip_gain, FLIP_Y_LO)
    gain = jnp.where(
        y_lo == 0, jnp.stack([skip_gain, other_gain]), jnp.stack([other_gain, skip_gain])
    )
    gated = (query * (convolved.astype(F32) + gain[:, :, None] * mixed)).astype(BF16)

    out_rows = lax.all_gather(out_proj, AXES, axis=0, axis_index_groups=groups)
    out_rows = out_rows.reshape(2, RINGS, 2, 64, 512)
    out_rows = jnp.concatenate([out_rows, out_rows], axis=1)
    out_rows = lax.dynamic_slice_in_dim(out_rows, z, RINGS, 1)
    out_kept = lax.dynamic_index_in_dim(out_rows, y_lo, 2, keepdims=False)
    out_given = lax.dynamic_index_in_dim(out_rows, 1 - y_lo, 2, keepdims=False)

    above, below = [gated], [gated]
    for _ in range(3):
        above.append(along_z(above[-1], -1))
        below.append(along_z(below[-1], 1))
    far = jnp.stack([along_z(below[3][0], 1), along_z(above[3][1], -1)])
    gathered = jnp.stack(above[:4] + [far] + below[3:0:-1], axis=1)

    def project(weights):
        return lax.dot_general(
            gathered.reshape(1024, half),
            weights.reshape(1024, 512),
            (((0,), (0,)), ((), ())),
            preferred_element_type=F32,
        ).astype(BF16)

    given = flip(project(out_given), FLIP_Y_LO)
    kept = project(out_kept)
    both = jnp.stack([kept, given])
    return jnp.where(y_lo == 0, both, both[::-1]).reshape(2 * half, 512)


def solution(mesh):
    placed = (
        P("ctx", "fsdp"),
        P(None, "fsdp", "ctx"),
        P("fsdp", "ctx"),
        P("fsdp"),
        P("ctx", "fsdp"),
    )
    return jax.shard_map(
        local, mesh=mesh, in_specs=placed, out_specs=P("ctx", "fsdp"), check_vma=False
    )
```

```python
import math

import jax
import jax.numpy as jnp
import numpy as np
from jax import lax
from jax.experimental import pallas as pl
from jax.experimental.pallas import tpu as pltpu
from jax.sharding import PartitionSpec as P

AXES = ("fsdp", "ctx")
RINGS = 8
SEQ = 32768
ROWS = 128
COLS = 256
F32 = jnp.float32
BF16 = jnp.bfloat16


def flip(array, mask):
    return lax.ppermute(array, AXES, [(i, i ^ mask) for i in range(256)])


FLIP_CORE = 1
FLIP_Y_HI = 2
FLIP_X = 4
FLIP_Y_LO = 128


def along_z(array, step):
    pairs = []
    for i in range(256):
        z = (i // 16) % RINGS
        pairs.append((i, i + 16 * ((z + step) % RINGS - z)))
    return lax.ppermute(array, AXES, pairs)


def plane_groups():
    return [
        [(y_lo * RINGS + z) * 16 + ctx for ctx in range(16) for y_lo in range(2)]
        for z in range(RINGS)
    ]


def transform_tables():
    freq = np.arange(ROWS)[:, None] + 0.25
    row_angle = 2.0 * np.pi * freq * np.arange(ROWS)[None, :] / ROWS
    twiddle_angle = 2.0 * np.pi * freq * np.arange(COLS)[None, :] / SEQ
    col_angle = 2.0 * np.pi * (np.arange(COLS)[:, None] * np.arange(COLS)[None, :] % COLS) / COLS
    cos_col, sin_col = np.cos(col_angle), np.sin(col_angle)
    row_forward = np.concatenate([np.cos(row_angle), -np.sin(row_angle)], axis=0)
    row_inverse = np.concatenate([np.cos(row_angle), -np.sin(row_angle)], axis=0).T / SEQ
    col_forward = np.block([[cos_col, -sin_col], [sin_col, cos_col]])
    col_inverse = np.block([[cos_col, sin_col], [-sin_col, cos_col]])
    twiddle = np.stack([np.cos(twiddle_angle), -np.sin(twiddle_angle)])
    return row_forward, row_inverse, col_forward, col_inverse, twiddle


def row_order(sources):
    per_source = ROWS // sources
    return (np.arange(sources)[None, :] * per_source + np.arange(per_source)[:, None]).reshape(-1)


def dot32(left, right):
    return jnp.dot(left, right, preferred_element_type=F32)


def forward(signal_ref, row_table, col_table, twiddle_ref):
    channels, sources, _ = signal_ref.shape
    per_source = ROWS // sources
    cos_part, sin_part = twiddle_ref[0], twiddle_ref[1]
    turned = []
    for channel in range(channels):
        signal = jnp.concatenate(
            [signal_ref[channel, :, pl.ds(j * COLS, COLS)] for j in range(per_source)], axis=0
        )
        both = dot32(row_table[...], signal)
        real, imag = both[:ROWS], both[ROWS:]
        turned.append(
            jnp.concatenate(
                [
                    (real * cos_part - imag * sin_part).astype(BF16),
                    (real * sin_part + imag * cos_part).astype(BF16),
                ],
                axis=1,
            )
        )
    return dot32(jnp.concatenate(turned, axis=0), col_table[...])


def filter_kernel(taps_ref, row_table, col_table, twiddle_ref, out_ref):
    out_ref[...] = forward(taps_ref, row_table, col_table, twiddle_ref)


def conv_kernel(
    signal_ref, spectrum_ref, row_table, col_table, col_back, row_back, twiddle_ref, out_ref
):
    channels, sources, _ = signal_ref.shape
    per_source = ROWS // sources
    spectrum = forward(signal_ref, row_table, col_table, twiddle_ref)
    real, imag = spectrum[:, :COLS], spectrum[:, COLS:]
    filter_real, filter_imag = spectrum_ref[:, :COLS], spectrum_ref[:, COLS:]
    product = jnp.concatenate(
        [
            (real * filter_real - imag * filter_imag).astype(BF16),
            (real * filter_imag + imag * filter_real).astype(BF16),
        ],
        axis=1,
    )
    back = dot32(product, col_back[...])
    cos_part, sin_part = twiddle_ref[0], twiddle_ref[1]
    for channel in range(channels):
        part = back[channel * ROWS : (channel + 1) * ROWS]
        real, imag = part[:, :COLS], part[:, COLS:]
        turned = jnp.concatenate(
            [
                (real * cos_part + imag * sin_part).astype(BF16),
                (imag * cos_part - real * sin_part).astype(BF16),
            ],
            axis=0,
        )
        result = dot32(row_back[...], turned).astype(BF16)
        for j in range(per_source):
            out_ref[channel, :, pl.ds(j * COLS, COLS)] = result[j * sources : (j + 1) * sources]


def call_local(kernel, out_shape, *operands):
    vmem = pl.BlockSpec(memory_space=pltpu.VMEM)
    return pl.pallas_call(
        kernel,
        out_shape=out_shape,
        in_specs=[vmem] * len(operands),
        out_specs=vmem,
        compiler_params=pltpu.CompilerParams(vmem_limit_bytes=24 * 1024 * 1024),
    )(*operands)


def x_groups():
    return [
        [fsdp * 16 + x * 4 + rest for x in range(4)] for fsdp in range(16) for rest in range(4)
    ]


def z_groups():
    return [list(range(first, first + RINGS)) for first in (0, RINGS)]


def after(array, *others):
    return lax.optimization_barrier((array,) + others)[0]


def gather_y(shard, y_hi):
    own = jnp.concatenate([shard, flip(shard, FLIP_Y_LO)], axis=-1)
    other = jnp.concatenate(
        [flip(shard, FLIP_Y_HI), flip(shard, FLIP_Y_HI | FLIP_Y_LO)], axis=-1
    )
    return jnp.where(y_hi == 0, jnp.stack([own, other]), jnp.stack([other, own]))


def gather_x(column):
    copies = jnp.broadcast_to(column[None], (4,) + column.shape)
    return lax.all_to_all(
        copies, AXES, split_axis=0, concat_axis=0, tiled=True, axis_index_groups=x_groups()
    )


def gather_core(plane, core):
    other = flip(plane, FLIP_CORE)
    both = jnp.where(core == 0, jnp.stack([plane, other], 2), jnp.stack([other, plane], 2))
    both = both.reshape((2, 2) + both.shape[1:])
    both = both.transpose((1, 2, 3, 0) + tuple(range(4, both.ndim)))
    return both.reshape((RINGS, 2) + both.shape[4:])


def reduce_over_z(parts):
    return lax.psum_scatter(
        parts, "fsdp", scatter_dimension=0, tiled=True, axis_index_groups=z_groups()
    )


def times_tokens(weights, wide_tokens):
    return lax.dot_general(
        weights.reshape(-1, 1024),
        wide_tokens,
        (((1,), (1,)), ((), ())),
        preferred_element_type=F32,
    ).astype(BF16)


def local(tokens, in_proj, filter_taps, skip_gain, out_proj):
    fsdp = lax.axis_index("fsdp")
    ctx = lax.axis_index("ctx")
    y_lo, z, y_hi, core = fsdp // RINGS, fsdp % RINGS, ctx // 2 % 2, ctx % 2
    groups = plane_groups()
    row_forward, row_inverse, col_forward, col_inverse, twiddle = transform_tables()
    as_bf16 = lambda table: jnp.asarray(table.astype(np.float32)).astype(BF16)
    twiddle = jnp.asarray(twiddle.astype(np.float32))
    half = tokens.shape[0] // 2

    shards = in_proj.transpose(0, 2, 1)
    given = lax.dynamic_slice_in_dim(tokens, (1 - y_lo) * half, half, 0)
    column = after(gather_y(shards[1:3], y_hi), given)

    plane = gather_x(column)
    got = flip(given, FLIP_Y_LO)
    other_gain = flip(skip_gain, FLIP_Y_LO)
    plane, got, other_gain, query_shard, out_proj = lax.optimization_barrier(
        (plane, got, other_gain, shards[0], out_proj)
    )
    gain = jnp.where(
        y_lo == 0, jnp.stack([skip_gain, other_gain]), jnp.stack([other_gain, skip_gain])
    )
    query_column = gather_y(query_shard, y_hi)
    out_other = flip(out_proj, FLIP_Y_HI)
    out_column = jnp.where(
        y_hi == 0, jnp.stack([out_proj, out_other]), jnp.stack([out_other, out_proj])
    )
    late = jnp.concatenate([query_column, out_column.reshape(2, 32, 1024)], axis=1)

    weights = gather_core(plane, core)
    kept = lax.dynamic_slice_in_dim(tokens, y_lo * half, half, 0)
    wide_tokens = jnp.concatenate([kept, got], axis=1)
    parts = times_tokens(weights, wide_tokens)
    sums = reduce_over_z(parts)

    late = gather_x(after(late, parts))
    late = gather_core(late, core)
    query_parts = times_tokens(late[:, :, :64], wide_tokens)
    query = reduce_over_z(query_parts)

    taps = after(filter_taps.astype(BF16), parts)
    taps = lax.all_to_all(
        taps.reshape(16, 4, 2048), "ctx", split_axis=0, concat_axis=0, tiled=True
    ).transpose(1, 0, 2)
    spectrum = call_local(
        filter_kernel,
        jax.ShapeDtypeStruct((4 * ROWS, 2 * COLS), F32),
        taps,
        as_bf16(row_forward[:, row_order(16)]),
        as_bf16(col_forward),
        twiddle,
    )
    sums, query_parts, spectrum = lax.optimization_barrier((sums, query_parts, spectrum))
    sums = sums.reshape(2, 2, 64, half).astype(F32)
    mixed = sums[:, 0] * sums[:, 1]

    def to_plane(array):
        return lax.all_to_all(
            array, AXES, split_axis=0, concat_axis=0, tiled=True, axis_index_groups=groups
        )

    spread = mixed.astype(BF16).reshape(2, 16, 4, half).transpose(1, 0, 2, 3).reshape(32, 4, half)
    spread = to_plane(spread).transpose(1, 0, 2)
    convolved = call_local(
        conv_kernel,
        jax.ShapeDtypeStruct(spread.shape, BF16),
        spread,
        spectrum,
        as_bf16(row_forward[:, row_order(32)]),
        as_bf16(col_forward),
        as_bf16(col_inverse),
        as_bf16(row_inverse[row_order(32)]),
        twiddle,
    )
    convolved = to_plane(convolved.transpose(1, 0, 2))
    convolved = convolved.reshape(16, 2, 4, half).transpose(1, 0, 2, 3).reshape(2, 64, half)

    query = query.reshape(2, 64, half).astype(F32)
    gated = (query * (convolved.astype(F32) + gain[:, :, None] * mixed)).astype(BF16)

    gated = gated.reshape(128, half)
    out_rows = late[:, :, 64:].reshape(1024, 512)

    def project(values):
        return lax.dot_general(
            values, out_rows, (((0,), (0,)), ((), ())), preferred_element_type=F32
        ).astype(BF16)

    gathered = lax.all_gather(
        gated, "fsdp", axis=0, tiled=True, axis_index_groups=z_groups()
    )
    up = down = flip(gated, FLIP_Y_LO)
    other_rows = jnp.zeros((1024, half), BF16)

    def put(array, piece, offset, row=0):
        return lax.dynamic_update_slice_in_dim(
            array, piece, (z + offset) % RINGS * 128 + row, 0
        )

    other_rows = put(other_rows, up, 0)
    for distance in (1, 2, 3):
        up, down = along_z(up, 1), along_z(down, -1)
        other_rows = put(put(other_rows, up, -distance), down, distance)
    up, down = along_z(up[:64], 1), along_z(down[64:], -1)
    other_rows = put(put(other_rows, up, -4), down, 4, 64)
    both = jnp.stack([project(gathered), project(other_rows)])
    return jnp.where(y_lo == 0, both, both[::-1]).reshape(2 * half, 512)


def solution(mesh):
    placed = (
        P("ctx", "fsdp"),
        P(None, "fsdp", "ctx"),
        P("fsdp", "ctx"),
        P("fsdp"),
        P("ctx", "fsdp"),
    )
    return jax.shard_map(
        local, mesh=mesh, in_specs=placed, out_specs=P("ctx", "fsdp"), check_vma=False
    )
```

```python
import math

import jax
import jax.numpy as jnp
import numpy as np
from jax import lax
from jax.experimental import pallas as pl
from jax.experimental.pallas import tpu as pltpu
from jax.sharding import PartitionSpec as P

AXES = ("fsdp", "ctx")
RINGS = 8
SEQ = 32768
ROWS = 128
COLS = 256
F32 = jnp.float32
BF16 = jnp.bfloat16


def flip(array, mask):
    return lax.ppermute(array, AXES, [(i, i ^ mask) for i in range(256)])


FLIP_CORE = 1
FLIP_Y_HI = 2
FLIP_X = 4
FLIP_Y_LO = 128


def along_z(array, step):
    pairs = []
    for i in range(256):
        z = (i // 16) % RINGS
        pairs.append((i, i + 16 * ((z + step) % RINGS - z)))
    return lax.ppermute(array, AXES, pairs)


def plane_groups():
    return [
        [(y_lo * RINGS + z) * 16 + ctx for ctx in range(16) for y_lo in range(2)]
        for z in range(RINGS)
    ]


def transform_tables():
    freq = np.arange(ROWS)[:, None] + 0.25
    row_angle = 2.0 * np.pi * freq * np.arange(ROWS)[None, :] / ROWS
    twiddle_angle = 2.0 * np.pi * freq * np.arange(COLS)[None, :] / SEQ
    col_angle = 2.0 * np.pi * (np.arange(COLS)[:, None] * np.arange(COLS)[None, :] % COLS) / COLS
    cos_col, sin_col = np.cos(col_angle), np.sin(col_angle)
    row_forward = np.concatenate([np.cos(row_angle), -np.sin(row_angle)], axis=0)
    row_inverse = np.concatenate([np.cos(row_angle), -np.sin(row_angle)], axis=0).T / SEQ
    col_forward = np.block([[cos_col, -sin_col], [sin_col, cos_col]])
    col_inverse = np.block([[cos_col, sin_col], [-sin_col, cos_col]])
    twiddle = np.stack([np.cos(twiddle_angle), -np.sin(twiddle_angle)])
    return row_forward, row_inverse, col_forward, col_inverse, twiddle


def row_order(sources):
    per_source = ROWS // sources
    return (np.arange(sources)[None, :] * per_source + np.arange(per_source)[:, None]).reshape(-1)


def dot32(left, right):
    return jnp.dot(left, right, preferred_element_type=F32)


def forward(signal_ref, row_table, col_table, twiddle_ref):
    channels, sources, _ = signal_ref.shape
    per_source = ROWS // sources
    cos_part, sin_part = twiddle_ref[0], twiddle_ref[1]
    turned = []
    for channel in range(channels):
        signal = jnp.concatenate(
            [signal_ref[channel, :, pl.ds(j * COLS, COLS)] for j in range(per_source)], axis=0
        )
        both = dot32(row_table[...], signal)
        real, imag = both[:ROWS], both[ROWS:]
        turned.append(
            jnp.concatenate(
                [
                    (real * cos_part - imag * sin_part).astype(BF16),
                    (real * sin_part + imag * cos_part).astype(BF16),
                ],
                axis=1,
            )
        )
    return dot32(jnp.concatenate(turned, axis=0), col_table[...])


def filter_kernel(taps_ref, row_table, col_table, twiddle_ref, out_ref):
    out_ref[...] = forward(taps_ref, row_table, col_table, twiddle_ref)


def conv_kernel(
    signal_ref, spectrum_ref, row_table, col_table, col_back, row_back, twiddle_ref, out_ref
):
    channels, sources, _ = signal_ref.shape
    per_source = ROWS // sources
    spectrum = forward(signal_ref, row_table, col_table, twiddle_ref)
    real, imag = spectrum[:, :COLS], spectrum[:, COLS:]
    filter_real, filter_imag = spectrum_ref[:, :COLS], spectrum_ref[:, COLS:]
    product = jnp.concatenate(
        [
            (real * filter_real - imag * filter_imag).astype(BF16),
            (real * filter_imag + imag * filter_real).astype(BF16),
        ],
        axis=1,
    )
    back = dot32(product, col_back[...])
    cos_part, sin_part = twiddle_ref[0], twiddle_ref[1]
    for channel in range(channels):
        part = back[channel * ROWS : (channel + 1) * ROWS]
        real, imag = part[:, :COLS], part[:, COLS:]
        turned = jnp.concatenate(
            [
                (real * cos_part + imag * sin_part).astype(BF16),
                (imag * cos_part - real * sin_part).astype(BF16),
            ],
            axis=0,
        )
        result = dot32(row_back[...], turned).astype(BF16)
        for j in range(per_source):
            out_ref[channel, :, pl.ds(j * COLS, COLS)] = result[j * sources : (j + 1) * sources]


def call_local(kernel, out_shape, *operands):
    vmem = pl.BlockSpec(memory_space=pltpu.VMEM)
    return pl.pallas_call(
        kernel,
        out_shape=out_shape,
        in_specs=[vmem] * len(operands),
        out_specs=vmem,
        compiler_params=pltpu.CompilerParams(vmem_limit_bytes=24 * 1024 * 1024),
    )(*operands)


def x_groups():
    return [
        [fsdp * 16 + x * 4 + rest for x in range(4)] for fsdp in range(16) for rest in range(4)
    ]


def z_groups():
    return [list(range(first, first + RINGS)) for first in (0, RINGS)]


def after(array, *others):
    return lax.optimization_barrier((array,) + others)[0]


def gather_y(shard, y_hi):
    own = jnp.concatenate([shard, flip(shard, FLIP_Y_LO)], axis=-1)
    other = jnp.concatenate(
        [flip(shard, FLIP_Y_HI), flip(shard, FLIP_Y_HI | FLIP_Y_LO)], axis=-1
    )
    return jnp.where(y_hi == 0, jnp.stack([own, other]), jnp.stack([other, own]))


def gather_x(column):
    copies = jnp.broadcast_to(column[None], (4,) + column.shape)
    return lax.all_to_all(
        copies, AXES, split_axis=0, concat_axis=0, tiled=True, axis_index_groups=x_groups()
    )


def product_kernel(core_ref, weights_ref, kept_ref, got_ref, *rest):
    del core_ref
    out_ref = rest[-1]
    width = kept_ref.shape[1]
    rows = weights_ref.shape[3]
    left = weights_ref[:, 0].reshape(4 * rows, 2 * width)
    over = (((1,), (1,)), ((), ()))
    sums = lax.dot_general(left[:, :width], kept_ref[...], over, preferred_element_type=F32)
    sums += lax.dot_general(left[:, width:], got_ref[...], over, preferred_element_type=F32)
    sums = sums.astype(BF16)
    for x_high in range(2):
        for y_high in range(2):
            first = (x_high * 2 + y_high) * rows
            out_ref[0, y_high, 0, x_high] = sums[first : first + rows]


def product(plane, rows, kept, got, core, *started):
    plane = plane.reshape(2, 2, 2, -1, 1024)
    count, width = kept.shape
    whole = pl.BlockSpec((count, width), lambda i, core: (0, 0))
    shape = (2, 2, 2, 2, rows, count)
    return pl.pallas_call(
        product_kernel,
        grid_spec=pltpu.PrefetchScalarGridSpec(
            num_scalar_prefetch=1,
            grid=(2,),
            in_specs=[
                pl.BlockSpec((2, 1, 2, rows, 1024), lambda i, core: (0, i, 0, 0, 0)),
                whole,
                whole,
            ]
            + [pl.BlockSpec(memory_space=pl.ANY)] * len(started),
            out_specs=pl.BlockSpec(
                (1, 2, 1, 2, rows, count), lambda i, core: (i, 0, core[0], 0, 0, 0)
            ),
        ),
        out_shape=pltpu.HBM(shape, BF16),
        input_output_aliases={4: 0} if started else {},
        compiler_params=pltpu.CompilerParams(vmem_limit_bytes=56 * 1024 * 1024),
        cost_estimate=pl.CostEstimate(
            flops=16 * rows * count * 1024, bytes_accessed=8 * 2**20, transcendentals=0
        ),
    )(jnp.reshape(core, (1,)).astype(jnp.int32), plane, kept, got, *started)


def products(plane, rows, kept, got, core):
    other = flip(plane, FLIP_CORE)
    own = product(plane, rows, kept, got, core)
    both = product(other, rows, kept, got, 1 - core, own)
    return both.reshape(-1, kept.shape[0]), other


def project_kernel(y_lo_ref, own_ref, other_ref, weights_ref, out_ref):
    del y_lo_ref
    over = (((0,), (0,)), ((), ()))

    def write(values_ref):
        out_ref[...] = lax.dot_general(
            values_ref[...], weights_ref[...], over, preferred_element_type=F32
        ).astype(BF16)

    first = pl.program_id(0) == 0
    pl.when(first)(lambda: write(own_ref))
    pl.when(jnp.logical_not(first))(lambda: write(other_ref))


def project(own, other, weights, y_lo):
    channels, count = own.shape
    features = weights.shape[1]
    block = count // 2
    return pl.pallas_call(
        project_kernel,
        grid_spec=pltpu.PrefetchScalarGridSpec(
            num_scalar_prefetch=1,
            grid=(2, 2),
            in_specs=[
                pl.BlockSpec((channels, block), lambda i, j, y: (0, jnp.where(i == 0, j, 1))),
                pl.BlockSpec((channels, block), lambda i, j, y: (0, jnp.where(i == 0, 0, j))),
                pl.BlockSpec((channels, features), lambda i, j, y: (0, 0)),
            ],
            out_specs=pl.BlockSpec(
                (block, features), lambda i, j, y: (jnp.where(i == 0, y[0], 1 - y[0]) * 2 + j, 0)
            ),
        ),
        out_shape=jax.ShapeDtypeStruct((2 * count, features), BF16),
        compiler_params=pltpu.CompilerParams(vmem_limit_bytes=56 * 1024 * 1024),
        cost_estimate=pl.CostEstimate(
            flops=4 * channels * count * features, bytes_accessed=7 * 2**20, transcendentals=0
        ),
    )(jnp.reshape(y_lo, (1,)).astype(jnp.int32), own, other, weights)


def reduce_over_z(parts):
    return lax.psum_scatter(
        parts, "fsdp", scatter_dimension=0, tiled=True, axis_index_groups=z_groups()
    )


def local(tokens, in_proj, filter_taps, skip_gain, out_proj):
    fsdp = lax.axis_index("fsdp")
    ctx = lax.axis_index("ctx")
    y_lo, z, y_hi, core = fsdp // RINGS, fsdp % RINGS, ctx // 2 % 2, ctx % 2
    groups = plane_groups()
    row_forward, row_inverse, col_forward, col_inverse, twiddle = transform_tables()
    as_bf16 = lambda table: jnp.asarray(table.astype(np.float32)).astype(BF16)
    twiddle = jnp.asarray(twiddle.astype(np.float32))
    half = tokens.shape[0] // 2

    shards = in_proj.transpose(0, 2, 1)
    given = lax.dynamic_slice_in_dim(tokens, (1 - y_lo) * half, half, 0)
    column = after(gather_y(shards[1:3], y_hi), given)

    plane = gather_x(column)
    got = flip(given, FLIP_Y_LO)
    other_gain = flip(skip_gain, FLIP_Y_LO)
    plane, got, other_gain, query_shard, out_proj = lax.optimization_barrier(
        (plane, got, other_gain, shards[0], out_proj)
    )
    gain = jnp.where(
        y_lo == 0, jnp.stack([skip_gain, other_gain]), jnp.stack([other_gain, skip_gain])
    )
    query_column = gather_y(query_shard, y_hi)
    out_other = flip(out_proj, FLIP_Y_HI)
    out_column = jnp.where(
        y_hi == 0, jnp.stack([out_proj, out_other]), jnp.stack([out_other, out_proj])
    )
    late = jnp.concatenate([query_column, out_column.reshape(2, 32, 1024)], axis=1)

    kept = lax.dynamic_slice_in_dim(tokens, y_lo * half, half, 0)
    parts, _ = products(plane, 128, kept, got, core)
    sums = reduce_over_z(parts)

    late = gather_x(after(late, parts))
    query_parts, other = products(late, 64, kept, got, core)
    query = reduce_over_z(query_parts)
    out_own, out_other = late[:, :, 64:], other[:, :, 64:]
    out_rows = jnp.where(
        core == 0, jnp.stack([out_own, out_other], 2), jnp.stack([out_other, out_own], 2)
    )
    out_rows = out_rows.reshape(2, 2, 2, 2, 64, 512).transpose(1, 2, 3, 0, 4, 5).reshape(1024, 512)

    taps = after(filter_taps.astype(BF16), parts)
    taps = lax.all_to_all(
        taps.reshape(16, 4, 2048), "ctx", split_axis=0, concat_axis=0, tiled=True
    ).transpose(1, 0, 2)
    spectrum = call_local(
        filter_kernel,
        jax.ShapeDtypeStruct((4 * ROWS, 2 * COLS), F32),
        taps,
        as_bf16(row_forward[:, row_order(16)]),
        as_bf16(col_forward),
        twiddle,
    )
    sums, query_parts, spectrum = lax.optimization_barrier((sums, query_parts, spectrum))
    sums = sums.reshape(2, 2, 64, half).astype(F32)
    mixed = sums[:, 0] * sums[:, 1]

    def to_plane(array):
        return lax.all_to_all(
            array, AXES, split_axis=0, concat_axis=0, tiled=True, axis_index_groups=groups
        )

    spread = mixed.astype(BF16).reshape(2, 16, 4, half).transpose(1, 0, 2, 3).reshape(32, 4, half)
    spread = to_plane(spread).transpose(1, 0, 2)
    convolved = call_local(
        conv_kernel,
        jax.ShapeDtypeStruct(spread.shape, BF16),
        spread,
        spectrum,
        as_bf16(row_forward[:, row_order(32)]),
        as_bf16(col_forward),
        as_bf16(col_inverse),
        as_bf16(row_inverse[row_order(32)]),
        twiddle,
    )
    convolved = to_plane(convolved.transpose(1, 0, 2))
    convolved = convolved.reshape(16, 2, 4, half).transpose(1, 0, 2, 3).reshape(2, 64, half)

    query = query.reshape(2, 64, half).astype(F32)
    gated = (query * (convolved.astype(F32) + gain[:, :, None] * mixed)).astype(BF16)

    gated = gated.reshape(128, half)

    gathered = lax.all_gather(
        gated, "fsdp", axis=0, tiled=True, axis_index_groups=z_groups()
    )
    up = down = flip(gated, FLIP_Y_LO)
    other_rows = jnp.zeros((1024, half), BF16)

    def put(array, piece, offset, row=0):
        return lax.dynamic_update_slice_in_dim(
            array, piece, (z + offset) % RINGS * 128 + row, 0
        )

    other_rows = put(other_rows, up, 0)
    for distance in (1, 2, 3):
        up, down = along_z(up, 1), along_z(down, -1)
        other_rows = put(put(other_rows, up, -distance), down, distance)
    up, down = along_z(up[:64], 1), along_z(down[64:], -1)
    other_rows = put(put(other_rows, up, -4), down, 4, 64)
    return project(gathered, other_rows, out_rows, y_lo)


def solution(mesh):
    placed = (
        P("ctx", "fsdp"),
        P(None, "fsdp", "ctx"),
        P("fsdp", "ctx"),
        P("fsdp"),
        P("ctx", "fsdp"),
    )
    return jax.shard_map(
        local, mesh=mesh, in_specs=placed, out_specs=P("ctx", "fsdp"), check_vma=False
    )
```

```python
import math

import jax
import jax.numpy as jnp
import numpy as np
from jax import lax
from jax.experimental import pallas as pl
from jax.experimental.pallas import tpu as pltpu
from jax.sharding import PartitionSpec as P

AXES = ("fsdp", "ctx")
RINGS = 8
SEQ = 32768
ROWS = 128
COLS = 256
F32 = jnp.float32
BF16 = jnp.bfloat16


def flip(array, mask):
    return lax.ppermute(array, AXES, [(i, i ^ mask) for i in range(256)])


FLIP_CORE = 1
FLIP_Y_HI = 2
FLIP_X = 4
FLIP_Y_LO = 128


def along_z(array, step):
    pairs = []
    for i in range(256):
        z = (i // 16) % RINGS
        pairs.append((i, i + 16 * ((z + step) % RINGS - z)))
    return lax.ppermute(array, AXES, pairs)


def plane_groups():
    return [
        [(y_lo * RINGS + z) * 16 + ctx for ctx in range(16) for y_lo in range(2)]
        for z in range(RINGS)
    ]


def transform_tables():
    freq = np.arange(ROWS)[:, None] + 0.25
    row_angle = 2.0 * np.pi * freq * np.arange(ROWS)[None, :] / ROWS
    twiddle_angle = 2.0 * np.pi * freq * np.arange(COLS)[None, :] / SEQ
    col_angle = 2.0 * np.pi * (np.arange(COLS)[:, None] * np.arange(COLS)[None, :] % COLS) / COLS
    cos_col, sin_col = np.cos(col_angle), np.sin(col_angle)
    row_forward = np.concatenate([np.cos(row_angle), -np.sin(row_angle)], axis=0)
    row_inverse = np.concatenate([np.cos(row_angle), -np.sin(row_angle)], axis=0).T / SEQ
    col_forward = np.block([[cos_col, -sin_col], [sin_col, cos_col]])
    col_inverse = np.block([[cos_col, sin_col], [-sin_col, cos_col]])
    twiddle = np.stack([np.cos(twiddle_angle), -np.sin(twiddle_angle)])
    return row_forward, row_inverse, col_forward, col_inverse, twiddle


def row_order(sources):
    per_source = ROWS // sources
    return (np.arange(sources)[None, :] * per_source + np.arange(per_source)[:, None]).reshape(-1)


def dot32(left, right):
    return jnp.dot(left, right, preferred_element_type=F32)


def forward(signal_ref, row_table, col_table, twiddle_ref):
    channels, sources, _ = signal_ref.shape
    per_source = ROWS // sources
    cos_part, sin_part = twiddle_ref[0], twiddle_ref[1]
    turned = []
    for channel in range(channels):
        signal = jnp.concatenate(
            [signal_ref[channel, :, pl.ds(j * COLS, COLS)] for j in range(per_source)], axis=0
        )
        both = dot32(row_table[...], signal)
        real, imag = both[:ROWS], both[ROWS:]
        turned.append(
            jnp.concatenate(
                [
                    (real * cos_part - imag * sin_part).astype(BF16),
                    (real * sin_part + imag * cos_part).astype(BF16),
                ],
                axis=1,
            )
        )
    return dot32(jnp.concatenate(turned, axis=0), col_table[...])


def filter_kernel(taps_ref, row_table, col_table, twiddle_ref, out_ref):
    out_ref[...] = forward(taps_ref, row_table, col_table, twiddle_ref)


def conv_kernel(
    signal_ref, spectrum_ref, row_table, col_table, col_back, row_back, twiddle_ref, out_ref
):
    channels, sources, _ = signal_ref.shape
    per_source = ROWS // sources
    spectrum = forward(signal_ref, row_table, col_table, twiddle_ref)
    real, imag = spectrum[:, :COLS], spectrum[:, COLS:]
    filter_real, filter_imag = spectrum_ref[:, :COLS], spectrum_ref[:, COLS:]
    product = jnp.concatenate(
        [
            (real * filter_real - imag * filter_imag).astype(BF16),
            (real * filter_imag + imag * filter_real).astype(BF16),
        ],
        axis=1,
    )
    back = dot32(product, col_back[...])
    cos_part, sin_part = twiddle_ref[0], twiddle_ref[1]
    for channel in range(channels):
        part = back[channel * ROWS : (channel + 1) * ROWS]
        real, imag = part[:, :COLS], part[:, COLS:]
        turned = jnp.concatenate(
            [
                (real * cos_part + imag * sin_part).astype(BF16),
                (imag * cos_part - real * sin_part).astype(BF16),
            ],
            axis=0,
        )
        result = dot32(row_back[...], turned).astype(BF16)
        for j in range(per_source):
            out_ref[channel, :, pl.ds(j * COLS, COLS)] = result[j * sources : (j + 1) * sources]


def call_local(kernel, out_shape, *operands):
    vmem = pl.BlockSpec(memory_space=pltpu.VMEM)
    return pl.pallas_call(
        kernel,
        out_shape=out_shape,
        in_specs=[vmem] * len(operands),
        out_specs=vmem,
        compiler_params=pltpu.CompilerParams(vmem_limit_bytes=24 * 1024 * 1024),
    )(*operands)


def x_groups():
    return [
        [fsdp * 16 + x * 4 + rest for x in range(4)] for fsdp in range(16) for rest in range(4)
    ]


def z_groups():
    return [list(range(first, first + RINGS)) for first in (0, RINGS)]


def after(array, *others):
    return lax.optimization_barrier((array,) + others)[0]


def gather_y(shard, y_hi):
    own = jnp.concatenate([shard, flip(shard, FLIP_Y_LO)], axis=-1)
    other = jnp.concatenate(
        [flip(shard, FLIP_Y_HI), flip(shard, FLIP_Y_HI | FLIP_Y_LO)], axis=-1
    )
    return jnp.where(y_hi == 0, jnp.stack([own, other]), jnp.stack([other, own]))


def gather_x(column):
    copies = jnp.broadcast_to(column[None], (4,) + column.shape)
    return lax.all_to_all(
        copies, AXES, split_axis=0, concat_axis=0, tiled=True, axis_index_groups=x_groups()
    )


def product_kernel(core_ref, weights_ref, kept_ref, got_ref, *rest):
    del core_ref
    out_ref = rest[-1]
    width = kept_ref.shape[1]
    rows = weights_ref.shape[3]
    left = weights_ref[:, 0].reshape(4 * rows, 2 * width)
    over = (((1,), (1,)), ((), ()))
    sums = lax.dot_general(left[:, :width], kept_ref[...], over, preferred_element_type=F32)
    sums += lax.dot_general(left[:, width:], got_ref[...], over, preferred_element_type=F32)
    sums = sums.astype(BF16)
    for x_high in range(2):
        for y_high in range(2):
            first = (x_high * 2 + y_high) * rows
            out_ref[0, y_high, 0, x_high] = sums[first : first + rows]


def product(plane, rows, kept, got, core, *started):
    plane = plane.reshape(2, 2, 2, -1, 1024)
    count, width = kept.shape
    whole = pl.BlockSpec((count, width), lambda i, core: (0, 0))
    shape = (2, 2, 2, 2, rows, count)
    return pl.pallas_call(
        product_kernel,
        grid_spec=pltpu.PrefetchScalarGridSpec(
            num_scalar_prefetch=1,
            grid=(2,),
            in_specs=[
                pl.BlockSpec((2, 1, 2, rows, 1024), lambda i, core: (0, i, 0, 0, 0)),
                whole,
                whole,
            ]
            + [pl.BlockSpec(memory_space=pl.ANY)] * len(started),
            out_specs=pl.BlockSpec(
                (1, 2, 1, 2, rows, count), lambda i, core: (i, 0, core[0], 0, 0, 0)
            ),
        ),
        out_shape=pltpu.HBM(shape, BF16),
        input_output_aliases={4: 0} if started else {},
        compiler_params=pltpu.CompilerParams(vmem_limit_bytes=32 * 1024 * 1024),
        cost_estimate=pl.CostEstimate(
            flops=16 * rows * count * 1024, bytes_accessed=8 * 2**20, transcendentals=0
        ),
    )(jnp.reshape(core, (1,)).astype(jnp.int32), plane, kept, got, *started)


def products(plane, rows, kept, got, core):
    other = flip(plane, FLIP_CORE)
    own = product(plane, rows, kept, got, core)
    both = product(other, rows, kept, got, 1 - core, own)
    return both.reshape(-1, kept.shape[0]), other


def project_kernel(y_lo_ref, own_ref, other_ref, weights_ref, out_ref):
    del y_lo_ref
    over = (((0,), (0,)), ((), ()))

    def write(values_ref):
        out_ref[...] = lax.dot_general(
            values_ref[...], weights_ref[...], over, preferred_element_type=F32
        ).astype(BF16)

    first = pl.program_id(0) == 0
    pl.when(first)(lambda: write(own_ref))
    pl.when(jnp.logical_not(first))(lambda: write(other_ref))


def project(own, other, weights, y_lo):
    channels, count = own.shape
    features = weights.shape[1]
    block = count // 2
    return pl.pallas_call(
        project_kernel,
        grid_spec=pltpu.PrefetchScalarGridSpec(
            num_scalar_prefetch=1,
            grid=(2, 2),
            in_specs=[
                pl.BlockSpec((channels, block), lambda i, j, y: (0, jnp.where(i == 0, j, 1))),
                pl.BlockSpec((channels, block), lambda i, j, y: (0, jnp.where(i == 0, 0, j))),
                pl.BlockSpec((channels, features), lambda i, j, y: (0, 0)),
            ],
            out_specs=pl.BlockSpec(
                (block, features), lambda i, j, y: (jnp.where(i == 0, y[0], 1 - y[0]) * 2 + j, 0)
            ),
        ),
        out_shape=jax.ShapeDtypeStruct((2 * count, features), BF16),
        compiler_params=pltpu.CompilerParams(vmem_limit_bytes=32 * 1024 * 1024),
        cost_estimate=pl.CostEstimate(
            flops=4 * channels * count * features, bytes_accessed=7 * 2**20, transcendentals=0
        ),
    )(jnp.reshape(y_lo, (1,)).astype(jnp.int32), own, other, weights)


def reduce_over_z(parts):
    return lax.psum_scatter(
        parts, "fsdp", scatter_dimension=0, tiled=True, axis_index_groups=z_groups()
    )


def local(tokens, in_proj, filter_taps, skip_gain, out_proj):
    fsdp = lax.axis_index("fsdp")
    ctx = lax.axis_index("ctx")
    y_lo, z, y_hi, core = fsdp // RINGS, fsdp % RINGS, ctx // 2 % 2, ctx % 2
    groups = plane_groups()
    row_forward, row_inverse, col_forward, col_inverse, twiddle = transform_tables()
    as_bf16 = lambda table: jnp.asarray(table.astype(np.float32)).astype(BF16)
    twiddle = jnp.asarray(twiddle.astype(np.float32))
    half = tokens.shape[0] // 2

    shards = in_proj.transpose(0, 2, 1)
    given = lax.dynamic_slice_in_dim(tokens, (1 - y_lo) * half, half, 0)
    column = after(gather_y(shards[1:3], y_hi), given)

    plane = gather_x(column)
    got = flip(given, FLIP_Y_LO)
    other_gain = flip(skip_gain, FLIP_Y_LO)
    plane, got, other_gain, query_shard, out_proj = lax.optimization_barrier(
        (plane, got, other_gain, shards[0], out_proj)
    )
    gain = jnp.where(
        y_lo == 0, jnp.stack([skip_gain, other_gain]), jnp.stack([other_gain, skip_gain])
    )
    query_column = gather_y(query_shard, y_hi)
    out_other = flip(out_proj, FLIP_Y_HI)
    out_column = jnp.where(
        y_hi == 0, jnp.stack([out_proj, out_other]), jnp.stack([out_other, out_proj])
    )
    late = jnp.concatenate([query_column, out_column.reshape(2, 32, 1024)], axis=1)

    kept = lax.dynamic_slice_in_dim(tokens, y_lo * half, half, 0)
    parts, _ = products(plane, 128, kept, got, core)
    sums = reduce_over_z(parts)

    late = gather_x(after(late, parts))
    query_parts, other = products(late, 64, kept, got, core)
    query = reduce_over_z(query_parts)
    out_own, out_other = late[:, :, 64:], other[:, :, 64:]
    out_rows = jnp.where(
        core == 0, jnp.stack([out_own, out_other], 2), jnp.stack([out_other, out_own], 2)
    )
    out_rows = out_rows.reshape(2, 2, 2, 2, 64, 512).transpose(1, 2, 3, 0, 4, 5).reshape(1024, 512)

    taps = after(filter_taps.astype(BF16), parts)
    taps = lax.all_to_all(
        taps.reshape(16, 4, 2048), "ctx", split_axis=0, concat_axis=0, tiled=True
    ).transpose(1, 0, 2)
    spectrum = call_local(
        filter_kernel,
        jax.ShapeDtypeStruct((4 * ROWS, 2 * COLS), F32),
        taps,
        as_bf16(row_forward[:, row_order(16)]),
        as_bf16(col_forward),
        twiddle,
    )
    sums, query_parts, spectrum = lax.optimization_barrier((sums, query_parts, spectrum))
    sums = sums.reshape(2, 2, 64, half).astype(F32)
    mixed = sums[:, 0] * sums[:, 1]

    def to_plane(array):
        return lax.all_to_all(
            array, AXES, split_axis=0, concat_axis=0, tiled=True, axis_index_groups=groups
        )

    spread = mixed.astype(BF16).reshape(2, 16, 4, half).transpose(1, 0, 2, 3).reshape(32, 4, half)
    spread = to_plane(spread).transpose(1, 0, 2)
    convolved = call_local(
        conv_kernel,
        jax.ShapeDtypeStruct(spread.shape, BF16),
        spread,
        spectrum,
        as_bf16(row_forward[:, row_order(32)]),
        as_bf16(col_forward),
        as_bf16(col_inverse),
        as_bf16(row_inverse[row_order(32)]),
        twiddle,
    )
    convolved = to_plane(convolved.transpose(1, 0, 2))
    convolved = convolved.reshape(16, 2, 4, half).transpose(1, 0, 2, 3).reshape(2, 64, half)

    query = query.reshape(2, 64, half).astype(F32)
    gated = (query * (convolved.astype(F32) + gain[:, :, None] * mixed)).astype(BF16)

    gated = gated.reshape(128, half)

    gathered = lax.all_gather(
        gated, "fsdp", axis=0, tiled=True, axis_index_groups=z_groups()
    )
    up = down = flip(gated, FLIP_Y_LO)
    other_rows = jnp.zeros((1024, half), BF16)

    def put(array, piece, offset, row=0):
        return lax.dynamic_update_slice_in_dim(
            array, piece, (z + offset) % RINGS * 128 + row, 0
        )

    other_rows = put(other_rows, up, 0)
    for distance in (1, 2, 3):
        up, down = along_z(up, 1), along_z(down, -1)
        other_rows = put(put(other_rows, up, -distance), down, distance)
    up, down = along_z(up[:64], 1), along_z(down[64:], -1)
    other_rows = put(put(other_rows, up, -4), down, 4, 64)
    return project(gathered, other_rows, out_rows, y_lo)


def solution(mesh):
    placed = (
        P("ctx", "fsdp"),
        P(None, "fsdp", "ctx"),
        P("fsdp", "ctx"),
        P("fsdp"),
        P("ctx", "fsdp"),
    )
    return jax.shard_map(
        local, mesh=mesh, in_specs=placed, out_specs=P("ctx", "fsdp"), check_vma=False
    )
```

```python
import math

import jax
import jax.numpy as jnp
import numpy as np
from jax import lax
from jax.experimental import pallas as pl
from jax.experimental.pallas import tpu as pltpu
from jax.sharding import PartitionSpec as P

AXES = ("fsdp", "ctx")
RINGS = 8
SEQ = 32768
ROWS = 128
COLS = 256
F32 = jnp.float32
BF16 = jnp.bfloat16


def flip(array, mask):
    return lax.ppermute(array, AXES, [(i, i ^ mask) for i in range(256)])


FLIP_CORE = 1
FLIP_Y_HI = 2
FLIP_X = 4
FLIP_Y_LO = 128


def along_z(array, step):
    pairs = []
    for i in range(256):
        z = (i // 16) % RINGS
        pairs.append((i, i + 16 * ((z + step) % RINGS - z)))
    return lax.ppermute(array, AXES, pairs)


def plane_groups():
    return [
        [(y_lo * RINGS + z) * 16 + ctx for ctx in range(16) for y_lo in range(2)]
        for z in range(RINGS)
    ]


def transform_tables():
    freq = np.arange(ROWS)[:, None] + 0.25
    row_angle = 2.0 * np.pi * freq * np.arange(ROWS)[None, :] / ROWS
    twiddle_angle = 2.0 * np.pi * freq * np.arange(COLS)[None, :] / SEQ
    col_angle = 2.0 * np.pi * (np.arange(COLS)[:, None] * np.arange(COLS)[None, :] % COLS) / COLS
    cos_col, sin_col = np.cos(col_angle), np.sin(col_angle)
    row_forward = np.concatenate([np.cos(row_angle), -np.sin(row_angle)], axis=0)
    row_inverse = np.concatenate([np.cos(row_angle), -np.sin(row_angle)], axis=0).T / SEQ
    col_forward = np.block([[cos_col, -sin_col], [sin_col, cos_col]])
    col_inverse = np.block([[cos_col, sin_col], [-sin_col, cos_col]])
    twiddle = np.stack([np.cos(twiddle_angle), -np.sin(twiddle_angle)])
    return row_forward, row_inverse, col_forward, col_inverse, twiddle


def row_order(sources):
    per_source = ROWS // sources
    return (np.arange(sources)[None, :] * per_source + np.arange(per_source)[:, None]).reshape(-1)


def dot32(left, right):
    return jnp.dot(left, right, preferred_element_type=F32)


def forward(signal_ref, row_table, col_table, twiddle_ref):
    channels, sources, _ = signal_ref.shape
    per_source = ROWS // sources
    cos_part, sin_part = twiddle_ref[0], twiddle_ref[1]
    turned = []
    for channel in range(channels):
        signal = jnp.concatenate(
            [signal_ref[channel, :, pl.ds(j * COLS, COLS)] for j in range(per_source)], axis=0
        )
        both = dot32(row_table[...], signal)
        real, imag = both[:ROWS], both[ROWS:]
        turned.append(
            jnp.concatenate(
                [
                    (real * cos_part - imag * sin_part).astype(BF16),
                    (real * sin_part + imag * cos_part).astype(BF16),
                ],
                axis=1,
            )
        )
    return dot32(jnp.concatenate(turned, axis=0), col_table[...])


def filter_kernel(taps_ref, row_table, col_table, twiddle_ref, out_ref):
    out_ref[...] = forward(taps_ref, row_table, col_table, twiddle_ref)


def conv_kernel(
    signal_ref, spectrum_ref, row_table, col_table, col_back, row_back, twiddle_ref, out_ref
):
    channels, sources, _ = signal_ref.shape
    per_source = ROWS // sources
    spectrum = forward(signal_ref, row_table, col_table, twiddle_ref)
    real, imag = spectrum[:, :COLS], spectrum[:, COLS:]
    filter_real, filter_imag = spectrum_ref[:, :COLS], spectrum_ref[:, COLS:]
    product = jnp.concatenate(
        [
            (real * filter_real - imag * filter_imag).astype(BF16),
            (real * filter_imag + imag * filter_real).astype(BF16),
        ],
        axis=1,
    )
    back = dot32(product, col_back[...])
    cos_part, sin_part = twiddle_ref[0], twiddle_ref[1]
    for channel in range(channels):
        part = back[channel * ROWS : (channel + 1) * ROWS]
        real, imag = part[:, :COLS], part[:, COLS:]
        turned = jnp.concatenate(
            [
                (real * cos_part + imag * sin_part).astype(BF16),
                (imag * cos_part - real * sin_part).astype(BF16),
            ],
            axis=0,
        )
        result = dot32(row_back[...], turned).astype(BF16)
        for j in range(per_source):
            out_ref[channel, :, pl.ds(j * COLS, COLS)] = result[j * sources : (j + 1) * sources]


def call_local(kernel, out_shape, *operands):
    vmem = pl.BlockSpec(memory_space=pltpu.VMEM)
    return pl.pallas_call(
        kernel,
        out_shape=out_shape,
        in_specs=[vmem] * len(operands),
        out_specs=vmem,
        compiler_params=pltpu.CompilerParams(vmem_limit_bytes=24 * 1024 * 1024),
    )(*operands)


def x_groups():
    return [
        [fsdp * 16 + x * 4 + rest for x in range(4)] for fsdp in range(16) for rest in range(4)
    ]


def z_groups():
    return [list(range(first, first + RINGS)) for first in (0, RINGS)]


def after(array, *others):
    return lax.optimization_barrier((array,) + others)[0]


def gather_y(shard, y_hi):
    own = jnp.concatenate([shard, flip(shard, FLIP_Y_LO)], axis=-1)
    other = jnp.concatenate(
        [flip(shard, FLIP_Y_HI), flip(shard, FLIP_Y_HI | FLIP_Y_LO)], axis=-1
    )
    return jnp.where(y_hi == 0, jnp.stack([own, other]), jnp.stack([other, own]))


def gather_x(column):
    copies = jnp.broadcast_to(column[None], (4,) + column.shape)
    return lax.all_to_all(
        copies, AXES, split_axis=0, concat_axis=0, tiled=True, axis_index_groups=x_groups()
    )


def product_kernel(core_ref, weights_ref, kept_ref, got_ref, *rest):
    del core_ref
    out_ref = rest[-1]
    width = kept_ref.shape[1]
    rows = weights_ref.shape[3]
    left = weights_ref[:, 0].reshape(4 * rows, 2 * width)
    over = (((1,), (1,)), ((), ()))
    sums = lax.dot_general(left[:, :width], kept_ref[...], over, preferred_element_type=F32)
    sums += lax.dot_general(left[:, width:], got_ref[...], over, preferred_element_type=F32)
    sums = sums.astype(BF16)
    for x_high in range(2):
        for y_high in range(2):
            first = (x_high * 2 + y_high) * rows
            out_ref[0, y_high, 0, x_high] = sums[first : first + rows]


def product(plane, rows, kept, got, core, *started):
    plane = plane.reshape(2, 2, 2, -1, 1024)
    count, width = kept.shape
    whole = pl.BlockSpec((count, width), lambda i, core: (0, 0))
    shape = (2, 2, 2, 2, rows, count)
    return pl.pallas_call(
        product_kernel,
        grid_spec=pltpu.PrefetchScalarGridSpec(
            num_scalar_prefetch=1,
            grid=(2,),
            in_specs=[
                pl.BlockSpec((2, 1, 2, rows, 1024), lambda i, core: (0, i, 0, 0, 0)),
                whole,
                whole,
            ]
            + [pl.BlockSpec(memory_space=pl.ANY)] * len(started),
            out_specs=pl.BlockSpec(
                (1, 2, 1, 2, rows, count), lambda i, core: (i, 0, core[0], 0, 0, 0)
            ),
        ),
        out_shape=pltpu.HBM(shape, BF16),
        input_output_aliases={4: 0} if started else {},
        compiler_params=pltpu.CompilerParams(vmem_limit_bytes=32 * 1024 * 1024),
        cost_estimate=pl.CostEstimate(
            flops=16 * rows * count * 1024, bytes_accessed=8 * 2**20, transcendentals=0
        ),
    )(jnp.reshape(core, (1,)).astype(jnp.int32), plane, kept, got, *started)


def products(plane, rows, kept, got, core):
    other = flip(plane, FLIP_CORE)
    own = product(plane, rows, kept, got, core)
    both = product(other, rows, kept, got, 1 - core, own)
    return both.reshape(-1, kept.shape[0]), other


def project_kernel(y_lo_ref, own_ref, other_ref, weights_ref, out_ref):
    del y_lo_ref
    over = (((0,), (0,)), ((), ()))

    def write(values_ref):
        out_ref[...] = lax.dot_general(
            values_ref[...], weights_ref[...], over, preferred_element_type=F32
        ).astype(BF16)

    first = pl.program_id(0) < 2
    pl.when(first)(lambda: write(own_ref))
    pl.when(jnp.logical_not(first))(lambda: write(other_ref))


def project(own, other, weights, y_lo):
    channels, count = own.shape
    features = weights.shape[1]
    block = count // 2
    return pl.pallas_call(
        project_kernel,
        grid_spec=pltpu.PrefetchScalarGridSpec(
            num_scalar_prefetch=1,
            grid=(3,),
            in_specs=[
                pl.BlockSpec((channels, block), lambda i, y: (0, jnp.minimum(i, 1))),
                pl.BlockSpec((channels, block), lambda i, y: (0, 0)),
                pl.BlockSpec((channels, features), lambda i, y: (0, 0)),
            ],
            out_specs=pl.BlockSpec(
                (block, features), lambda i, y: (jnp.where(i < 2, y[0] * 2 + i, (1 - y[0]) * 2), 0)
            ),
        ),
        out_shape=pltpu.HBM((2 * count, features), BF16),
        compiler_params=pltpu.CompilerParams(vmem_limit_bytes=32 * 1024 * 1024),
        cost_estimate=pl.CostEstimate(
            flops=3 * channels * count * features, bytes_accessed=6 * 2**20, transcendentals=0
        ),
    )(jnp.reshape(y_lo, (1,)).astype(jnp.int32), own, other, weights)


def reduce_over_z(parts):
    return lax.psum_scatter(
        parts, "fsdp", scatter_dimension=0, tiled=True, axis_index_groups=z_groups()
    )


def local(tokens, in_proj, filter_taps, skip_gain, out_proj):
    fsdp = lax.axis_index("fsdp")
    ctx = lax.axis_index("ctx")
    y_lo, z, y_hi, core = fsdp // RINGS, fsdp % RINGS, ctx // 2 % 2, ctx % 2
    groups = plane_groups()
    row_forward, row_inverse, col_forward, col_inverse, twiddle = transform_tables()
    as_bf16 = lambda table: jnp.asarray(table.astype(np.float32)).astype(BF16)
    twiddle = jnp.asarray(twiddle.astype(np.float32))
    half = tokens.shape[0] // 2

    shards = in_proj.transpose(0, 2, 1)
    given = lax.dynamic_slice_in_dim(tokens, (1 - y_lo) * half, half, 0)
    column = after(gather_y(shards[1:3], y_hi), given)

    plane = gather_x(column)
    got = flip(given, FLIP_Y_LO)
    other_gain = flip(skip_gain, FLIP_Y_LO)
    plane, got, other_gain, query_shard, out_proj = lax.optimization_barrier(
        (plane, got, other_gain, shards[0], out_proj)
    )
    gain = jnp.where(
        y_lo == 0, jnp.stack([skip_gain, other_gain]), jnp.stack([other_gain, skip_gain])
    )
    query_column = gather_y(query_shard, y_hi)
    late = jnp.concatenate([query_column, gather_y(out_proj, y_hi)], axis=1)

    kept = lax.dynamic_slice_in_dim(tokens, y_lo * half, half, 0)
    parts, _ = products(plane, 128, kept, got, core)
    sums = reduce_over_z(parts)

    late = gather_x(after(late, parts))
    query_parts, other = products(late, 64, kept, got, core)
    query = reduce_over_z(query_parts)
    out_own, out_other = late[:, :, 64:], other[:, :, 64:]
    out_rows = jnp.where(
        core == 0, jnp.stack([out_own, out_other], 2), jnp.stack([out_other, out_own], 2)
    )
    out_rows = out_rows.reshape(2, 2, 2, 2, 64, 1024).transpose(1, 2, 3, 0, 4, 5).reshape(1024, 1024)

    taps = after(filter_taps.astype(BF16), parts)
    taps = lax.all_to_all(
        taps.reshape(16, 4, 2048), "ctx", split_axis=0, concat_axis=0, tiled=True
    ).transpose(1, 0, 2)
    spectrum = call_local(
        filter_kernel,
        jax.ShapeDtypeStruct((4 * ROWS, 2 * COLS), F32),
        taps,
        as_bf16(row_forward[:, row_order(16)]),
        as_bf16(col_forward),
        twiddle,
    )
    sums, query_parts, spectrum = lax.optimization_barrier((sums, query_parts, spectrum))
    sums = sums.reshape(2, 2, 64, half).astype(F32)
    mixed = sums[:, 0] * sums[:, 1]

    def to_plane(array):
        return lax.all_to_all(
            array, AXES, split_axis=0, concat_axis=0, tiled=True, axis_index_groups=groups
        )

    spread = mixed.astype(BF16).reshape(2, 16, 4, half).transpose(1, 0, 2, 3).reshape(32, 4, half)
    spread = to_plane(spread).transpose(1, 0, 2)
    convolved = call_local(
        conv_kernel,
        jax.ShapeDtypeStruct(spread.shape, BF16),
        spread,
        spectrum,
        as_bf16(row_forward[:, row_order(32)]),
        as_bf16(col_forward),
        as_bf16(col_inverse),
        as_bf16(row_inverse[row_order(32)]),
        twiddle,
    )
    convolved = to_plane(convolved.transpose(1, 0, 2))
    convolved = convolved.reshape(16, 2, 4, half).transpose(1, 0, 2, 3).reshape(2, 64, half)

    query = query.reshape(2, 64, half).astype(F32)
    gated = (query * (convolved.astype(F32) + gain[:, :, None] * mixed)).astype(BF16)

    gated = gated.reshape(128, half)
    quarter = half // 2

    def put(array, piece, offset, row=0):
        return lax.dynamic_update_slice_in_dim(
            array, piece, (z + offset) % RINGS * 128 + row, 0
        )

    other_rows = lax.all_gather(
        flip(gated[:, :quarter], FLIP_Y_LO),
        "fsdp",
        axis=0,
        tiled=True,
        axis_index_groups=z_groups(),
    )
    up = down = gated
    own_rows = put(query_parts, gated, 0)
    for distance in (1, 2, 3):
        up, down = along_z(up, 1), along_z(down, -1)
        own_rows = put(put(own_rows, up, -distance), down, distance)
    up, down = along_z(up[:64], 1), along_z(down[64:], -1)
    own_rows = put(put(own_rows, up, -4), down, 4, 64)
    given = lax.dot_general(
        own_rows[:, quarter:],
        out_rows[:, 512:],
        (((0,), (0,)), ((), ())),
        preferred_element_type=F32,
    ).astype(BF16)
    got = flip(given, FLIP_Y_LO)
    result = project(own_rows, other_rows, out_rows[:, :512], y_lo)
    return lax.dynamic_update_slice_in_dim(result, got, (1 - y_lo) * half + quarter, 0)


def solution(mesh):
    placed = (
        P("ctx", "fsdp"),
        P(None, "fsdp", "ctx"),
        P("fsdp", "ctx"),
        P("fsdp"),
        P("ctx", "fsdp"),
    )
    return jax.shard_map(
        local, mesh=mesh, in_specs=placed, out_specs=P("ctx", "fsdp"), check_vma=False
    )
```

```python
import math

import jax
import jax.numpy as jnp
import numpy as np
from jax import lax
from jax.experimental import pallas as pl
from jax.experimental.pallas import tpu as pltpu
from jax.sharding import PartitionSpec as P

AXES = ("fsdp", "ctx")
RINGS = 8
SEQ = 32768
ROWS = 128
COLS = 256
F32 = jnp.float32
BF16 = jnp.bfloat16


def flip(array, mask):
    return lax.ppermute(array, AXES, [(i, i ^ mask) for i in range(256)])


FLIP_CORE = 1
FLIP_Y_HI = 2
FLIP_X = 4
FLIP_Y_LO = 128


def along_z(array, step):
    pairs = []
    for i in range(256):
        z = (i // 16) % RINGS
        pairs.append((i, i + 16 * ((z + step) % RINGS - z)))
    return lax.ppermute(array, AXES, pairs)


def plane_groups():
    return [
        [(y_lo * RINGS + z) * 16 + ctx for ctx in range(16) for y_lo in range(2)]
        for z in range(RINGS)
    ]


def transform_tables():
    freq = np.arange(ROWS)[:, None] + 0.25
    row_angle = 2.0 * np.pi * freq * np.arange(ROWS)[None, :] / ROWS
    twiddle_angle = 2.0 * np.pi * freq * np.arange(COLS)[None, :] / SEQ
    col_angle = 2.0 * np.pi * (np.arange(COLS)[:, None] * np.arange(COLS)[None, :] % COLS) / COLS
    cos_col, sin_col = np.cos(col_angle), np.sin(col_angle)
    row_forward = np.concatenate([np.cos(row_angle), -np.sin(row_angle)], axis=0)
    row_inverse = np.concatenate([np.cos(row_angle), -np.sin(row_angle)], axis=0).T / SEQ
    col_forward = np.block([[cos_col, -sin_col], [sin_col, cos_col]])
    col_inverse = np.block([[cos_col, sin_col], [-sin_col, cos_col]])
    twiddle = np.stack([np.cos(twiddle_angle), -np.sin(twiddle_angle)])
    return row_forward, row_inverse, col_forward, col_inverse, twiddle


def row_order(sources):
    per_source = ROWS // sources
    return (np.arange(sources)[None, :] * per_source + np.arange(per_source)[:, None]).reshape(-1)


def dot32(left, right):
    return jnp.dot(left, right, preferred_element_type=F32)


def forward(signal_ref, row_table, col_table, twiddle_ref):
    channels, sources, _ = signal_ref.shape
    per_source = ROWS // sources
    cos_part, sin_part = twiddle_ref[0], twiddle_ref[1]
    turned = []
    for channel in range(channels):
        signal = jnp.concatenate(
            [signal_ref[channel, :, pl.ds(j * COLS, COLS)] for j in range(per_source)], axis=0
        )
        both = dot32(row_table[...], signal)
        real, imag = both[:ROWS], both[ROWS:]
        turned.append(
            jnp.concatenate(
                [
                    (real * cos_part - imag * sin_part).astype(BF16),
                    (real * sin_part + imag * cos_part).astype(BF16),
                ],
                axis=1,
            )
        )
    return dot32(jnp.concatenate(turned, axis=0), col_table[...])


def filter_kernel(taps_ref, row_table, col_table, twiddle_ref, out_ref):
    out_ref[...] = forward(taps_ref, row_table, col_table, twiddle_ref)


def conv_kernel(
    signal_ref, spectrum_ref, row_table, col_table, col_back, row_back, twiddle_ref, out_ref
):
    channels, sources, _ = signal_ref.shape
    per_source = ROWS // sources
    spectrum = forward(signal_ref, row_table, col_table, twiddle_ref)
    real, imag = spectrum[:, :COLS], spectrum[:, COLS:]
    filter_real, filter_imag = spectrum_ref[:, :COLS], spectrum_ref[:, COLS:]
    product = jnp.concatenate(
        [
            (real * filter_real - imag * filter_imag).astype(BF16),
            (real * filter_imag + imag * filter_real).astype(BF16),
        ],
        axis=1,
    )
    back = dot32(product, col_back[...])
    cos_part, sin_part = twiddle_ref[0], twiddle_ref[1]
    for channel in range(channels):
        part = back[channel * ROWS : (channel + 1) * ROWS]
        real, imag = part[:, :COLS], part[:, COLS:]
        turned = jnp.concatenate(
            [
                (real * cos_part + imag * sin_part).astype(BF16),
                (imag * cos_part - real * sin_part).astype(BF16),
            ],
            axis=0,
        )
        result = dot32(row_back[...], turned).astype(BF16)
        for j in range(per_source):
            out_ref[channel, :, pl.ds(j * COLS, COLS)] = result[j * sources : (j + 1) * sources]


def call_local(kernel, out_shape, *operands):
    vmem = pl.BlockSpec(memory_space=pltpu.VMEM)
    return pl.pallas_call(
        kernel,
        out_shape=out_shape,
        in_specs=[vmem] * len(operands),
        out_specs=vmem,
        compiler_params=pltpu.CompilerParams(vmem_limit_bytes=24 * 1024 * 1024),
    )(*operands)


def x_groups():
    return [
        [fsdp * 16 + x * 4 + rest for x in range(4)] for fsdp in range(16) for rest in range(4)
    ]


def z_groups():
    return [list(range(first, first + RINGS)) for first in (0, RINGS)]


def after(array, *others):
    return lax.optimization_barrier((array,) + others)[0]


def gather_y(shard, y_hi):
    own = jnp.concatenate([shard, flip(shard, FLIP_Y_LO)], axis=-1)
    other = jnp.concatenate(
        [flip(shard, FLIP_Y_HI), flip(shard, FLIP_Y_HI | FLIP_Y_LO)], axis=-1
    )
    return jnp.where(y_hi == 0, jnp.stack([own, other]), jnp.stack([other, own]))


def gather_x(column):
    copies = jnp.broadcast_to(column[None], (4,) + column.shape)
    return lax.all_to_all(
        copies, AXES, split_axis=0, concat_axis=0, tiled=True, axis_index_groups=x_groups()
    )


def product_kernel(core_ref, weights_ref, kept_ref, got_ref, *rest):
    del core_ref
    out_ref = rest[-1]
    width = kept_ref.shape[1]
    rows = weights_ref.shape[3]
    left = weights_ref[:, 0].reshape(4 * rows, 2 * width)
    over = (((1,), (1,)), ((), ()))
    sums = lax.dot_general(left[:, :width], kept_ref[...], over, preferred_element_type=F32)
    sums += lax.dot_general(left[:, width:], got_ref[...], over, preferred_element_type=F32)
    sums = sums.astype(BF16)
    for x_high in range(2):
        for y_high in range(2):
            first = (x_high * 2 + y_high) * rows
            out_ref[0, y_high, 0, x_high] = sums[first : first + rows]


def product(plane, rows, kept, got, core, *started):
    plane = plane.reshape(2, 2, 2, -1, 1024)
    count, width = kept.shape
    whole = pl.BlockSpec((count, width), lambda i, core: (0, 0))
    shape = (2, 2, 2, 2, rows, count)
    return pl.pallas_call(
        product_kernel,
        grid_spec=pltpu.PrefetchScalarGridSpec(
            num_scalar_prefetch=1,
            grid=(2,),
            in_specs=[
                pl.BlockSpec((2, 1, 2, rows, 1024), lambda i, core: (0, i, 0, 0, 0)),
                whole,
                whole,
            ]
            + [pl.BlockSpec(memory_space=pl.ANY)] * len(started),
            out_specs=pl.BlockSpec(
                (1, 2, 1, 2, rows, count), lambda i, core: (i, 0, core[0], 0, 0, 0)
            ),
        ),
        out_shape=pltpu.HBM(shape, BF16),
        input_output_aliases={4: 0} if started else {},
        compiler_params=pltpu.CompilerParams(vmem_limit_bytes=32 * 1024 * 1024),
        cost_estimate=pl.CostEstimate(
            flops=16 * rows * count * 1024, bytes_accessed=8 * 2**20, transcendentals=0
        ),
    )(jnp.reshape(core, (1,)).astype(jnp.int32), plane, kept, got, *started)


def products(plane, rows, kept, got, core):
    other = flip(plane, FLIP_CORE)
    own = product(plane, rows, kept, got, core)
    both = product(other, rows, kept, got, 1 - core, own)
    return both.reshape(-1, kept.shape[0]), other


def project_kernel(y_lo_ref, values_ref, weights_ref, *rest):
    del y_lo_ref
    out_ref = rest[-1]

    def multiply():
        out_ref[...] = lax.dot_general(
            values_ref[...],
            weights_ref[...],
            (((0,), (0,)), ((), ())),
            preferred_element_type=F32,
        ).astype(BF16)

    def copy():
        out_ref[...] = rest[0][...]

    if len(rest) == 1:
        multiply()
    else:
        first = pl.program_id(0) == 0
        pl.when(first)(multiply)
        pl.when(jnp.logical_not(first))(copy)


def project(values, weights, y_lo, rows, *more):
    channels, block = values.shape[0], rows // 4
    if more:
        place = lambda i, y: ((1 - y[0]) * 2 + i, 0)
        chosen = lambda i, y: (0, 0)
        extra = [
            pl.BlockSpec((block, 512), lambda i, y: (0, 0)),
            pl.BlockSpec(memory_space=pl.ANY),
        ]
    else:
        place = lambda i, y: (y[0] * 2 + i, 0)
        chosen = lambda i, y: (0, i)
        extra = []
    return pl.pallas_call(
        project_kernel,
        grid_spec=pltpu.PrefetchScalarGridSpec(
            num_scalar_prefetch=1,
            grid=(2,),
            in_specs=[
                pl.BlockSpec((channels, block), chosen),
                pl.BlockSpec((channels, 512), lambda i, y: (0, 0)),
            ]
            + extra,
            out_specs=pl.BlockSpec((block, 512), place),
        ),
        out_shape=pltpu.HBM((rows, 512), BF16),
        input_output_aliases={4: 0} if more else {},
        compiler_params=pltpu.CompilerParams(vmem_limit_bytes=32 * 1024 * 1024),
        cost_estimate=pl.CostEstimate(
            flops=2 * channels * block * 512, bytes_accessed=3 * 2**20, transcendentals=0
        ),
    )(jnp.reshape(y_lo, (1,)).astype(jnp.int32), values, weights, *more)


def reduce_over_z(parts):
    return lax.psum_scatter(
        parts, "fsdp", scatter_dimension=0, tiled=True, axis_index_groups=z_groups()
    )


def local(tokens, in_proj, filter_taps, skip_gain, out_proj):
    fsdp = lax.axis_index("fsdp")
    ctx = lax.axis_index("ctx")
    y_lo, z, y_hi, core = fsdp // RINGS, fsdp % RINGS, ctx // 2 % 2, ctx % 2
    groups = plane_groups()
    row_forward, row_inverse, col_forward, col_inverse, twiddle = transform_tables()
    as_bf16 = lambda table: jnp.asarray(table.astype(np.float32)).astype(BF16)
    twiddle = jnp.asarray(twiddle.astype(np.float32))
    half = tokens.shape[0] // 2

    shards = in_proj.transpose(0, 2, 1)
    given = lax.dynamic_slice_in_dim(tokens, (1 - y_lo) * half, half, 0)
    column = after(gather_y(shards[1:3], y_hi), given)

    plane = gather_x(column)
    got = flip(given, FLIP_Y_LO)
    other_gain = flip(skip_gain, FLIP_Y_LO)
    plane, got, other_gain, query_shard, out_proj = lax.optimization_barrier(
        (plane, got, other_gain, shards[0], out_proj)
    )
    gain = jnp.where(
        y_lo == 0, jnp.stack([skip_gain, other_gain]), jnp.stack([other_gain, skip_gain])
    )
    query_column = gather_y(query_shard, y_hi)
    late = jnp.concatenate([query_column, gather_y(out_proj, y_hi)], axis=1)

    kept = lax.dynamic_slice_in_dim(tokens, y_lo * half, half, 0)
    parts, _ = products(plane, 128, kept, got, core)
    sums = reduce_over_z(parts)

    late = gather_x(after(late, parts))
    query_parts, other = products(late, 64, kept, got, core)
    query = reduce_over_z(query_parts)
    out_own, out_other = late[:, :, 64:], other[:, :, 64:]
    out_rows = jnp.where(
        core == 0, jnp.stack([out_own, out_other], 2), jnp.stack([out_other, out_own], 2)
    )
    out_rows = out_rows.reshape(2, 2, 2, 2, 64, 1024).transpose(1, 2, 3, 0, 4, 5).reshape(1024, 1024)

    taps = after(filter_taps.astype(BF16), parts)
    taps = lax.all_to_all(
        taps.reshape(16, 4, 2048), "ctx", split_axis=0, concat_axis=0, tiled=True
    ).transpose(1, 0, 2)
    spectrum = call_local(
        filter_kernel,
        jax.ShapeDtypeStruct((4 * ROWS, 2 * COLS), F32),
        taps,
        as_bf16(row_forward[:, row_order(16)]),
        as_bf16(col_forward),
        twiddle,
    )
    sums, query_parts, spectrum = lax.optimization_barrier((sums, query_parts, spectrum))
    sums = sums.reshape(2, 2, 64, half).astype(F32)
    mixed = sums[:, 0] * sums[:, 1]

    def to_plane(array):
        return lax.all_to_all(
            array, AXES, split_axis=0, concat_axis=0, tiled=True, axis_index_groups=groups
        )

    spread = mixed.astype(BF16).reshape(2, 16, 4, half).transpose(1, 0, 2, 3).reshape(32, 4, half)
    spread = to_plane(spread).transpose(1, 0, 2)
    convolved = call_local(
        conv_kernel,
        jax.ShapeDtypeStruct(spread.shape, BF16),
        spread,
        spectrum,
        as_bf16(row_forward[:, row_order(32)]),
        as_bf16(col_forward),
        as_bf16(col_inverse),
        as_bf16(row_inverse[row_order(32)]),
        twiddle,
    )
    convolved = to_plane(convolved.transpose(1, 0, 2))
    convolved = convolved.reshape(16, 2, 4, half).transpose(1, 0, 2, 3).reshape(2, 64, half)

    query = query.reshape(2, 64, half).astype(F32)
    gated = (query * (convolved.astype(F32) + gain[:, :, None] * mixed)).astype(BF16)

    gated = gated.reshape(128, half)
    quarter = half // 2

    def put(array, piece, offset, row=0):
        return lax.dynamic_update_slice_in_dim(
            array, piece, (z + offset) % RINGS * 128 + row, 0
        )

    other_rows = lax.all_gather(
        flip(gated[:, :quarter], FLIP_Y_LO),
        "fsdp",
        axis=0,
        tiled=True,
        axis_index_groups=z_groups(),
    )
    up = down = gated
    own_rows = put(query_parts, gated, 0)
    for distance in (1, 2, 3):
        up, down = along_z(up, 1), along_z(down, -1)
        own_rows = put(put(own_rows, up, -distance), down, distance)
    up, down = along_z(up[:64], 1), along_z(down[64:], -1)
    own_rows = put(put(own_rows, up, -4), down, 4, 64)
    given = lax.dot_general(
        own_rows[:, quarter:],
        out_rows[:, 512:],
        (((0,), (0,)), ((), ())),
        preferred_element_type=F32,
    ).astype(BF16)
    got = flip(given, FLIP_Y_LO)
    result = project(own_rows, out_rows, y_lo, 2 * half)
    return project(other_rows, out_rows, y_lo, 2 * half, got, result)


def solution(mesh):
    placed = (
        P("ctx", "fsdp"),
        P(None, "fsdp", "ctx"),
        P("fsdp", "ctx"),
        P("fsdp"),
        P("ctx", "fsdp"),
    )
    return jax.shard_map(
        local, mesh=mesh, in_specs=placed, out_specs=P("ctx", "fsdp"), check_vma=False
    )
```

```python
import math

import jax
import jax.numpy as jnp
import numpy as np
from jax import lax
from jax.experimental import pallas as pl
from jax.experimental.pallas import tpu as pltpu
from jax.sharding import PartitionSpec as P

AXES = ("fsdp", "ctx")
RINGS = 8
SEQ = 32768
ROWS = 128
COLS = 256
F32 = jnp.float32
BF16 = jnp.bfloat16


def flip(array, mask):
    return lax.ppermute(array, AXES, [(i, i ^ mask) for i in range(256)])


FLIP_CORE = 1
FLIP_Y_HI = 2
FLIP_X = 4
FLIP_Y_LO = 128


def along_z(array, step):
    pairs = []
    for i in range(256):
        z = (i // 16) % RINGS
        pairs.append((i, i + 16 * ((z + step) % RINGS - z)))
    return lax.ppermute(array, AXES, pairs)


def plane_groups():
    return [
        [(y_lo * RINGS + z) * 16 + ctx for ctx in range(16) for y_lo in range(2)]
        for z in range(RINGS)
    ]


def transform_tables():
    freq = np.arange(ROWS)[:, None] + 0.25
    row_angle = 2.0 * np.pi * freq * np.arange(ROWS)[None, :] / ROWS
    twiddle_angle = 2.0 * np.pi * freq * np.arange(COLS)[None, :] / SEQ
    col_angle = 2.0 * np.pi * (np.arange(COLS)[:, None] * np.arange(COLS)[None, :] % COLS) / COLS
    cos_col, sin_col = np.cos(col_angle), np.sin(col_angle)
    row_forward = np.concatenate([np.cos(row_angle), -np.sin(row_angle)], axis=0)
    row_inverse = np.concatenate([np.cos(row_angle), -np.sin(row_angle)], axis=0).T / SEQ
    col_forward = np.block([[cos_col, -sin_col], [sin_col, cos_col]])
    col_inverse = np.block([[cos_col, sin_col], [-sin_col, cos_col]])
    twiddle = np.stack([np.cos(twiddle_angle), -np.sin(twiddle_angle)])
    return row_forward, row_inverse, col_forward, col_inverse, twiddle


def row_order(sources):
    per_source = ROWS // sources
    return (np.arange(sources)[None, :] * per_source + np.arange(per_source)[:, None]).reshape(-1)


def dot32(left, right):
    return jnp.dot(left, right, preferred_element_type=F32)


def forward(signal_ref, row_table, col_table, twiddle_ref):
    channels, sources, _ = signal_ref.shape
    per_source = ROWS // sources
    cos_part, sin_part = twiddle_ref[0], twiddle_ref[1]
    turned = []
    for channel in range(channels):
        signal = jnp.concatenate(
            [signal_ref[channel, :, pl.ds(j * COLS, COLS)] for j in range(per_source)], axis=0
        )
        both = dot32(row_table[...], signal)
        real, imag = both[:ROWS], both[ROWS:]
        turned.append(
            jnp.concatenate(
                [
                    (real * cos_part - imag * sin_part).astype(BF16),
                    (real * sin_part + imag * cos_part).astype(BF16),
                ],
                axis=1,
            )
        )
    return dot32(jnp.concatenate(turned, axis=0), col_table[...])


def filter_kernel(taps_ref, row_table, col_table, twiddle_ref, out_ref):
    out_ref[...] = forward(taps_ref, row_table, col_table, twiddle_ref)


def conv_kernel(
    signal_ref, spectrum_ref, row_table, col_table, col_back, row_back, twiddle_ref, out_ref
):
    channels, sources, _ = signal_ref.shape
    per_source = ROWS // sources
    spectrum = forward(signal_ref, row_table, col_table, twiddle_ref)
    real, imag = spectrum[:, :COLS], spectrum[:, COLS:]
    filter_real, filter_imag = spectrum_ref[:, :COLS], spectrum_ref[:, COLS:]
    product = jnp.concatenate(
        [
            (real * filter_real - imag * filter_imag).astype(BF16),
            (real * filter_imag + imag * filter_real).astype(BF16),
        ],
        axis=1,
    )
    back = dot32(product, col_back[...])
    cos_part, sin_part = twiddle_ref[0], twiddle_ref[1]
    for channel in range(channels):
        part = back[channel * ROWS : (channel + 1) * ROWS]
        real, imag = part[:, :COLS], part[:, COLS:]
        turned = jnp.concatenate(
            [
                (real * cos_part + imag * sin_part).astype(BF16),
                (imag * cos_part - real * sin_part).astype(BF16),
            ],
            axis=0,
        )
        result = dot32(row_back[...], turned).astype(BF16)
        for j in range(per_source):
            out_ref[channel, :, pl.ds(j * COLS, COLS)] = result[j * sources : (j + 1) * sources]


def call_local(kernel, out_shape, *operands):
    vmem = pl.BlockSpec(memory_space=pltpu.VMEM)
    return pl.pallas_call(
        kernel,
        out_shape=out_shape,
        in_specs=[vmem] * len(operands),
        out_specs=vmem,
        compiler_params=pltpu.CompilerParams(vmem_limit_bytes=24 * 1024 * 1024),
    )(*operands)


def x_groups():
    return [
        [fsdp * 16 + x * 4 + rest for x in range(4)] for fsdp in range(16) for rest in range(4)
    ]


def z_groups():
    return [list(range(first, first + RINGS)) for first in (0, RINGS)]


def after(array, *others):
    return lax.optimization_barrier((array,) + others)[0]


def gather_y(shard, y_hi):
    own = jnp.concatenate([shard, flip(shard, FLIP_Y_LO)], axis=-1)
    other = jnp.concatenate(
        [flip(shard, FLIP_Y_HI), flip(shard, FLIP_Y_HI | FLIP_Y_LO)], axis=-1
    )
    return jnp.where(y_hi == 0, jnp.stack([own, other]), jnp.stack([other, own]))


def gather_x(column):
    copies = jnp.broadcast_to(column[None], (4,) + column.shape)
    return lax.all_to_all(
        copies, AXES, split_axis=0, concat_axis=0, tiled=True, axis_index_groups=x_groups()
    )


def product_kernel(core_ref, weights_ref, kept_ref, got_ref, *rest):
    del core_ref
    out_ref = rest[-1]
    width = kept_ref.shape[1]
    rows = weights_ref.shape[3]
    left = weights_ref[:, 0].reshape(4 * rows, 2 * width)
    over = (((1,), (1,)), ((), ()))
    sums = lax.dot_general(left[:, :width], kept_ref[...], over, preferred_element_type=F32)
    sums += lax.dot_general(left[:, width:], got_ref[...], over, preferred_element_type=F32)
    sums = sums.astype(BF16)
    for x_high in range(2):
        for y_high in range(2):
            first = (x_high * 2 + y_high) * rows
            out_ref[0, y_high, 0, x_high] = sums[first : first + rows]


def product(plane, rows, kept, got, core, *started):
    plane = plane.reshape(2, 2, 2, -1, 1024)
    count, width = kept.shape
    whole = pl.BlockSpec((count, width), lambda i, core: (0, 0))
    shape = (2, 2, 2, 2, rows, count)
    return pl.pallas_call(
        product_kernel,
        grid_spec=pltpu.PrefetchScalarGridSpec(
            num_scalar_prefetch=1,
            grid=(2,),
            in_specs=[
                pl.BlockSpec((2, 1, 2, rows, 1024), lambda i, core: (0, i, 0, 0, 0)),
                whole,
                whole,
            ]
            + [pl.BlockSpec(memory_space=pl.ANY)] * len(started),
            out_specs=pl.BlockSpec(
                (1, 2, 1, 2, rows, count), lambda i, core: (i, 0, core[0], 0, 0, 0)
            ),
        ),
        out_shape=pltpu.HBM(shape, BF16),
        input_output_aliases={4: 0} if started else {},
        compiler_params=pltpu.CompilerParams(vmem_limit_bytes=32 * 1024 * 1024),
        cost_estimate=pl.CostEstimate(
            flops=16 * rows * count * 1024, bytes_accessed=8 * 2**20, transcendentals=0
        ),
    )(jnp.reshape(core, (1,)).astype(jnp.int32), plane, kept, got, *started)


def products(plane, rows, kept, got, core):
    other = flip(plane, FLIP_CORE)
    own = product(plane, rows, kept, got, core)
    both = product(other, rows, kept, got, 1 - core, own)
    return both.reshape(-1, kept.shape[0]), other


def project_kernel(y_lo_ref, values_ref, weights_ref, *rest):
    del y_lo_ref
    out_ref = rest[-1]

    def multiply():
        out_ref[...] = lax.dot_general(
            values_ref[...],
            weights_ref[...],
            (((0,), (0,)), ((), ())),
            preferred_element_type=F32,
        ).astype(BF16)

    def copy():
        out_ref[...] = rest[0][...]

    if len(rest) == 1:
        multiply()
    else:
        first = pl.program_id(0) == 0
        pl.when(first)(multiply)
        pl.when(jnp.logical_not(first))(copy)


def project(values, weights, y_lo, rows, *more):
    channels, block = values.shape[0], rows // 4
    if more:
        place = lambda i, y: ((1 - y[0]) * 2 + i, 0)
        chosen = lambda i, y: (0, 0)
        extra = [
            pl.BlockSpec((block, 512), lambda i, y: (0, 0)),
            pl.BlockSpec(memory_space=pl.ANY),
        ]
    else:
        place = lambda i, y: (y[0] * 2 + i, 0)
        chosen = lambda i, y: (0, i)
        extra = []
    return pl.pallas_call(
        project_kernel,
        grid_spec=pltpu.PrefetchScalarGridSpec(
            num_scalar_prefetch=1,
            grid=(2,),
            in_specs=[
                pl.BlockSpec((channels, block), chosen),
                pl.BlockSpec((channels, 512), lambda i, y: (0, 0)),
            ]
            + extra,
            out_specs=pl.BlockSpec((block, 512), place),
        ),
        out_shape=pltpu.HBM((rows, 512), BF16),
        input_output_aliases={4: 0} if more else {},
        compiler_params=pltpu.CompilerParams(vmem_limit_bytes=32 * 1024 * 1024),
        cost_estimate=pl.CostEstimate(
            flops=2 * channels * block * 512, bytes_accessed=3 * 2**20, transcendentals=0
        ),
    )(jnp.reshape(y_lo, (1,)).astype(jnp.int32), values, weights, *more)


def reduce_over_z(parts):
    return lax.psum_scatter(
        parts, "fsdp", scatter_dimension=0, tiled=True, axis_index_groups=z_groups()
    )


def local(tokens, in_proj, filter_taps, skip_gain, out_proj):
    fsdp = lax.axis_index("fsdp")
    ctx = lax.axis_index("ctx")
    y_lo, z, y_hi, core = fsdp // RINGS, fsdp % RINGS, ctx // 2 % 2, ctx % 2
    groups = plane_groups()
    row_forward, row_inverse, col_forward, col_inverse, twiddle = transform_tables()
    as_bf16 = lambda table: jnp.asarray(table.astype(np.float32)).astype(BF16)
    twiddle = jnp.asarray(twiddle.astype(np.float32))
    half = tokens.shape[0] // 2

    shards = in_proj.transpose(0, 2, 1)
    given = lax.dynamic_slice_in_dim(tokens, (1 - y_lo) * half, half, 0)
    column = gather_y(shards[1:3], y_hi)

    plane = gather_x(column)
    got = flip(given, FLIP_Y_LO)
    other_gain = flip(skip_gain, FLIP_Y_LO)
    plane, got, other_gain, query_shard, out_proj = lax.optimization_barrier(
        (plane, got, other_gain, shards[0], out_proj)
    )
    gain = jnp.where(
        y_lo == 0, jnp.stack([skip_gain, other_gain]), jnp.stack([other_gain, skip_gain])
    )
    query_column = gather_y(query_shard, y_hi)
    late = jnp.concatenate([query_column, gather_y(out_proj, y_hi)], axis=1)

    kept = lax.dynamic_slice_in_dim(tokens, y_lo * half, half, 0)
    parts, _ = products(plane, 128, kept, got, core)
    sums = reduce_over_z(parts)

    late = gather_x(after(late, parts))
    query_parts, other = products(late, 64, kept, got, core)
    query = reduce_over_z(query_parts)
    out_own, out_other = late[:, :, 64:], other[:, :, 64:]
    out_rows = jnp.where(
        core == 0, jnp.stack([out_own, out_other], 2), jnp.stack([out_other, out_own], 2)
    )
    out_rows = out_rows.reshape(2, 2, 2, 2, 64, 1024).transpose(1, 2, 3, 0, 4, 5).reshape(1024, 1024)

    taps = after(filter_taps.astype(BF16), parts)
    taps = lax.all_to_all(
        taps.reshape(16, 4, 2048), "ctx", split_axis=0, concat_axis=0, tiled=True
    ).transpose(1, 0, 2)
    spectrum = call_local(
        filter_kernel,
        jax.ShapeDtypeStruct((4 * ROWS, 2 * COLS), F32),
        taps,
        as_bf16(row_forward[:, row_order(16)]),
        as_bf16(col_forward),
        twiddle,
    )
    sums, query_parts, spectrum = lax.optimization_barrier((sums, query_parts, spectrum))
    sums = sums.reshape(2, 2, 64, half).astype(F32)
    mixed = sums[:, 0] * sums[:, 1]

    def to_plane(array):
        return lax.all_to_all(
            array, AXES, split_axis=0, concat_axis=0, tiled=True, axis_index_groups=groups
        )

    spread = mixed.astype(BF16).reshape(2, 16, 4, half).transpose(1, 0, 2, 3).reshape(32, 4, half)
    spread = to_plane(spread).transpose(1, 0, 2)
    convolved = call_local(
        conv_kernel,
        jax.ShapeDtypeStruct(spread.shape, BF16),
        spread,
        spectrum,
        as_bf16(row_forward[:, row_order(32)]),
        as_bf16(col_forward),
        as_bf16(col_inverse),
        as_bf16(row_inverse[row_order(32)]),
        twiddle,
    )
    convolved = to_plane(convolved.transpose(1, 0, 2))
    convolved = convolved.reshape(16, 2, 4, half).transpose(1, 0, 2, 3).reshape(2, 64, half)

    query = query.reshape(2, 64, half).astype(F32)
    gated = (query * (convolved.astype(F32) + gain[:, :, None] * mixed)).astype(BF16)

    gated = gated.reshape(128, half)
    quarter = half // 2

    def put(array, piece, offset, row=0):
        return lax.dynamic_update_slice_in_dim(
            array, piece, (z + offset) % RINGS * 128 + row, 0
        )

    other_rows = lax.all_gather(
        flip(gated[:, :quarter], FLIP_Y_LO),
        "fsdp",
        axis=0,
        tiled=True,
        axis_index_groups=z_groups(),
    )
    up = down = gated
    own_rows = put(query_parts, gated, 0)
    for distance in (1, 2, 3):
        up, down = along_z(up, 1), along_z(down, -1)
        own_rows = put(put(own_rows, up, -distance), down, distance)
    up, down = along_z(up[:64], 1), along_z(down[64:], -1)
    own_rows = put(put(own_rows, up, -4), down, 4, 64)
    given = lax.dot_general(
        own_rows[:, quarter:],
        out_rows[:, 512:],
        (((0,), (0,)), ((), ())),
        preferred_element_type=F32,
    ).astype(BF16)
    got = flip(given, FLIP_Y_LO)
    result = project(own_rows, out_rows, y_lo, 2 * half)
    return project(other_rows, out_rows, y_lo, 2 * half, got, result)


def solution(mesh):
    placed = (
        P("ctx", "fsdp"),
        P(None, "fsdp", "ctx"),
        P("fsdp", "ctx"),
        P("fsdp"),
        P("ctx", "fsdp"),
    )
    return jax.shard_map(
        local, mesh=mesh, in_specs=placed, out_specs=P("ctx", "fsdp"), check_vma=False
    )
```
